512 devices in a mesh: row: 32 (over y, z_hi, core), col: 16 (over z_lo, x).
Axes of the slice: x: 4, y: 8, z: 8 (z_hi: 2, z_lo: 4; z = z_hi * 4 + z_lo), core: 2. Of those that a mesh axis runs over, the one named last changes fastest.
Arguments:
- queries: bfloat16 [512, 128, 1536], P('row', 'col'), may hold values from -8 to 8
- keys: bfloat16 [512, 128, 1536], P('row', 'col'), may hold values from -8 to 8
- values: bfloat16 [512, 128, 1536], P('row', 'col'), may hold values from -6 to 6
- out_grad: bfloat16 [512, 128, 1536], P('row', 'col'), may hold values from -15 to 15
Outputs:
- qkv_grad: bfloat16 [512, 128, 4608], P('row', 'col')
The draws below stay inside these ranges and needn't reach their ends.
All inputs are finite; a program needn't handle non-finite values.
Results may differ from the reference program's by a relative error of at most 0.007.
Values may be sent and summed in bfloat16 or wider, within the bound.
A program may use at most 128 MiB of HBM per device.

```python
import math
import jax
import jax.numpy as jnp
from jax import lax

HEAD_DIM = 128
HEADS = 12
RADIUS = 8
TR = 16
TC = 8
CH = 1536
NR = 512
NC = 128


def draw_queries(key, part):
    key = jax.random.fold_in(key, 7)
    base = jnp.clip(jax.random.normal(key, (NR, NC, CH), jnp.float32), -6.0, 6.0)
    return base.astype(jnp.bfloat16)


def draw_keys(key, part):
    key = jax.random.fold_in(key, 9)
    base = jnp.clip(jax.random.normal(key, (NR, NC, CH), jnp.float32), -6.0, 6.0)
    return base.astype(jnp.bfloat16)


def block_scale(rng, extent, cuts, smallest, top_value):
    loudness = 1.0
    for axis_at, shards_of in cuts:
        steps = jax.random.uniform(jax.random.fold_in(jax.random.fold_in(rng, 6), axis_at), (shards_of,), jnp.float32, smallest / len(cuts), top_value / len(cuts))
        loudness = loudness * jnp.repeat(jnp.exp(steps), extent[axis_at] // shards_of).reshape((-1,) + (1,) * (len(extent) - 1 - axis_at))
    return loudness


def centred(stream_key, dims, spread, reach, split=(), kind=jnp.bfloat16):
    loudness = block_scale(stream_key, dims, split, -0.22, 0.18) if split else 1.0
    drawn = jax.random.normal(stream_key, dims, jnp.float32) * spread * loudness
    return jnp.minimum(jnp.maximum(drawn, -reach), reach).astype(kind)


def setup_inputs(seed: int = 0) -> dict:
    splits = jax.random.split(jax.random.key(seed), 5)
    return {
        "queries": draw_queries(jax.random.fold_in(splits[4], 71), 0),
        "keys": draw_keys(jax.random.fold_in(splits[4], 71), 0),
        "values": centred(splits[2], (NR, NC, CH), 1.0, 6.0, ((0, 32), (1, 16))),
        "out_grad": centred(splits[3], (NR, NC, CH), 5.0, 15.0, ((0, 32), (1, 16))),
    }


FLOOR = -1e+30

def pair_mask(query_rows, query_cols, key_rows, key_cols, grid_rows, grid_cols):
    query_row_in = (query_rows >= 0) & (query_rows < grid_rows)
    query_col_in = (query_cols >= 0) & (query_cols < grid_cols)
    key_row_in = (key_rows >= 0) & (key_rows < grid_rows)
    key_col_in = (key_cols >= 0) & (key_cols < grid_cols)
    row_match = (jnp.abs(query_rows[:, None] - key_rows[None, :]) <= RADIUS) & query_row_in[:, None] & key_row_in[None, :]
    col_match = (jnp.abs(query_cols[:, None] - key_cols[None, :]) <= RADIUS) & query_col_in[:, None] & key_col_in[None, :]
    joined = row_match[:, None, :, None] & col_match[None, :, None, :]
    return joined.reshape(query_rows.shape[0] * query_cols.shape[0], key_rows.shape[0] * key_cols.shape[0])

def split_heads(block):
    return block.reshape(-1, block.shape[-1] // HEAD_DIM, HEAD_DIM).astype(jnp.float32)

def to_grid(stat, grid_shape):
    return jnp.transpose(stat[:, :, 0]).reshape(grid_shape[0], grid_shape[1], -1)

def query_terms(query_heads, key_heads, value_heads, grad_heads, mask, scale_factor):
    scores = jnp.einsum('qhd,khd->hqk', query_heads, key_heads) * scale_factor
    masked = jnp.where(mask[None], scores, FLOOR)
    peak = lax.optimization_barrier(jnp.max(masked, axis=2, keepdims=True))
    log_total = peak + jnp.log(lax.optimization_barrier(jnp.sum(jnp.exp(masked - peak), axis=2, keepdims=True)))
    weights = jnp.exp(masked - log_total)
    grad_prob = jnp.einsum('qhd,khd->hqk', grad_heads, value_heads)
    offset = lax.optimization_barrier(jnp.sum(weights * grad_prob, axis=2, keepdims=True))
    grad_score = (weights * (grad_prob - offset)).astype(jnp.bfloat16)
    return (weights, grad_score, log_total, offset)

def key_terms(query_heads, grad_heads, log_total, offset, key_heads, value_heads, mask, scale_factor):
    scores = jnp.einsum('qhd,khd->hqk', query_heads, key_heads) * scale_factor
    masked = jnp.where(mask[None], scores, FLOOR)
    weights = jnp.exp(masked - log_total)
    grad_prob = jnp.einsum('qhd,khd->hqk', grad_heads, value_heads)
    grad_score = (weights * (grad_prob - offset)).astype(jnp.bfloat16)
    key_grad = jnp.einsum('hqk,qhd->khd', grad_score.astype(jnp.float32), query_heads) * scale_factor
    value_grad = jnp.einsum('hqk,qhd->khd', weights.astype(jnp.bfloat16).astype(jnp.float32), grad_heads)
    return (key_grad, value_grad)

def reference(queries, keys, values, out_grad):
    scale_factor = 1.0 / math.sqrt(HEAD_DIM)
    tiles_across = NC // TC
    tile_count = NR // TR * tiles_across
    border = ((RADIUS, RADIUS), (RADIUS, RADIUS), (0, 0))
    outer_rows_n = TR + 2 * RADIUS
    outer_cols_n = TC + 2 * RADIUS
    keys_pad = jnp.pad(keys, border)
    values_pad = jnp.pad(values, border)

    def places(index):
        row_start = index // tiles_across * TR
        col_start = index % tiles_across * TC
        own_rows = row_start + jnp.arange(TR, dtype=jnp.int32)
        own_cols = col_start + jnp.arange(TC, dtype=jnp.int32)
        outer_rows = row_start - RADIUS + jnp.arange(outer_rows_n, dtype=jnp.int32)
        outer_cols = col_start - RADIUS + jnp.arange(outer_cols_n, dtype=jnp.int32)
        return (row_start, col_start, own_rows, own_cols, outer_rows, outer_cols)

    def query_pass(index):
        row_start, col_start, own_rows, own_cols, outer_rows, outer_cols = places(index)
        zero = row_start * 0
        query_block = lax.dynamic_slice(queries, (row_start, col_start, zero), (TR, TC, CH))
        grad_block = lax.dynamic_slice(out_grad, (row_start, col_start, zero), (TR, TC, CH))
        key_block = lax.dynamic_slice(keys_pad, (row_start, col_start, zero), (outer_rows_n, outer_cols_n, CH))
        value_block = lax.dynamic_slice(values_pad, (row_start, col_start, zero), (outer_rows_n, outer_cols_n, CH))
        mask = pair_mask(own_rows, own_cols, outer_rows, outer_cols, NR, NC)
        key_heads = split_heads(key_block)
        weights, grad_score, log_total, offset = query_terms(split_heads(query_block), key_heads, split_heads(value_block), split_heads(grad_block), mask, scale_factor)
        query_grad = jnp.einsum('hqk,khd->qhd', grad_score.astype(jnp.float32), key_heads) * scale_factor
        query_grad = query_grad.astype(jnp.bfloat16).reshape(TR, TC, CH)
        return (query_grad, to_grid(log_total, (TR, TC)), to_grid(offset, (TR, TC)))

    def untile(stacked):
        shaped = stacked.reshape(NR // TR, tiles_across, TR, TC, -1)
        return jnp.transpose(shaped, (0, 2, 1, 3, 4)).reshape(NR, NC, -1)
    query_grads, totals, offsets = lax.map(query_pass, jnp.arange(tile_count, dtype=jnp.int32))
    query_grad = untile(query_grads)
    total_pad = jnp.pad(untile(totals), border)
    offset_pad = jnp.pad(untile(offsets), border)
    queries_pad = jnp.pad(queries, border)
    grads_pad = jnp.pad(out_grad, border)

    def key_pass(index):
        row_start, col_start, own_rows, own_cols, outer_rows, outer_cols = places(index)
        zero = row_start * 0
        key_block = lax.dynamic_slice(keys, (row_start, col_start, zero), (TR, TC, CH))
        value_block = lax.dynamic_slice(values, (row_start, col_start, zero), (TR, TC, CH))
        query_block = lax.dynamic_slice(queries_pad, (row_start, col_start, zero), (outer_rows_n, outer_cols_n, CH))
        grad_block = lax.dynamic_slice(grads_pad, (row_start, col_start, zero), (outer_rows_n, outer_cols_n, CH))
        total_block = lax.dynamic_slice(total_pad, (row_start, col_start, zero), (outer_rows_n, outer_cols_n, HEADS))
        offset_block = lax.dynamic_slice(offset_pad, (row_start, col_start, zero), (outer_rows_n, outer_cols_n, HEADS))
        mask = pair_mask(outer_rows, outer_cols, own_rows, own_cols, NR, NC)
        outer_total = jnp.transpose(total_block.reshape(-1, HEADS))[:, :, None]
        outer_offset = jnp.transpose(offset_block.reshape(-1, HEADS))[:, :, None]
        key_grad, value_grad = key_terms(split_heads(query_block), split_heads(grad_block), outer_total, outer_offset, split_heads(key_block), split_heads(value_block), mask, scale_factor)
        return (key_grad.astype(jnp.bfloat16).reshape(TR, TC, CH), value_grad.astype(jnp.bfloat16).reshape(TR, TC, CH))
    key_grads, value_grads = lax.map(key_pass, jnp.arange(tile_count, dtype=jnp.int32))
    return jnp.concatenate([query_grad, untile(key_grads), untile(value_grads)], axis=2)
```

```python
import functools
import math

import jax
import jax.numpy as jnp
from jax import lax
from jax.experimental import pallas as pl
from jax.experimental.pallas import tpu as pltpu
from jax.sharding import PartitionSpec as P

HEAD_DIM = 128
RADIUS = 8
TILE_ROWS = 16
TILE_COLS = 8
TOKENS = TILE_ROWS * TILE_COLS
CELL = 64
BLOCK = 2 * TOKENS
WINDOW = 3 * BLOCK
FLOOR = -1e30
MESH = pl.DeviceIdType.MESH
LOOK = 2

OUT, SIB, LEFT, RIGHT, OUT_LEFT, OUT_RIGHT, SIB_LEFT, SIB_RIGHT = range(8)


def dot(a, b, dims):
    return lax.dot_general(a, b, (dims, ((), ())), preferred_element_type=jnp.float32)


def fill_bias(bias, row, col, grid_rows, grid_cols):
    own = lax.broadcasted_iota(jnp.int32, (TOKENS, TOKENS), 0)
    lane = lax.broadcasted_iota(jnp.int32, (TOKENS, TOKENS), 1)
    own_row, own_col = own >> 3, own & 7
    for block in range(3):
        for half in range(2):
            if half == 0:
                key_row = lane >> 3
            else:
                key_row = jnp.where(lane < CELL, 16 + (lane >> 3), (lane >> 3) - 16)
            key_col = (lane & 7) + (block - 1) * TILE_COLS
            grid_row = key_row + row * TILE_ROWS
            grid_col = key_col + col * TILE_COLS
            ok = (
                (jnp.abs(own_row - key_row) <= RADIUS)
                & (jnp.abs(own_col - key_col) <= RADIUS)
                & (grid_row >= 0)
                & (grid_row < grid_rows)
                & (grid_col >= 0)
                & (grid_col < grid_cols)
            )
            start = block * BLOCK + half * TOKENS
            bias[:, start : start + TOKENS] = jnp.where(ok, 0.0, FLOOR)


def kernel(
    heads, rows, cols,
    q_ref, k_ref, v_ref, g_ref, out_ref,
    win, bias, stat_out, stat_in, load_sem, send_sem, recv_sem, stat_send, stat_recv,
):
    row, col = lax.axis_index("row"), lax.axis_index("col")
    core = lax.rem(row, 2)
    outside = row - 1 + 2 * core
    sibling = row + 1 - 2 * core
    has_out = (outside >= 0) & (outside < rows)
    has_left = col > 0
    has_right = col < cols - 1
    has_up = row > 0
    has_down = row < rows - 1
    around = []
    for dr in (-1, 0, 1):
        for dc in (-1, 0, 1):
            if dr == 0 and dc == 0:
                continue
            there = None
            for cond in ([has_up, None, has_down][dr + 1], [has_left, None, has_right][dc + 1]):
                if cond is not None:
                    there = cond if there is None else there & cond
            around.append((dr, dc, there))

    loads = []
    for a, ref in enumerate((q_ref, k_ref, v_ref, g_ref)):
        copy = pltpu.make_async_copy(ref, win.at[a, pl.ds(BLOCK, TOKENS)], load_sem.at[a])
        copy.start()
        loads.append(copy)

    barrier = pltpu.get_barrier_semaphore()
    for dr, dc, there in around:
        @pl.when(there)
        def _():
            pl.semaphore_signal(barrier, inc=1, device_id=(row + dr, col + dc), device_id_type=MESH)
    n_rows = 1 + has_up.astype(jnp.int32) + has_down.astype(jnp.int32)
    n_cols = 1 + has_left.astype(jnp.int32) + has_right.astype(jnp.int32)
    pl.semaphore_wait(barrier, n_rows * n_cols - 1)
    for copy in loads:
        copy.wait()

    far = 1 - core
    out_slot = pl.multiple_of(TOKENS + far * CELL, CELL)
    sib_slot = pl.multiple_of(TOKENS + core * CELL, CELL)

    def lanes(k):
        return pl.ds(pl.multiple_of(k * HEAD_DIM, HEAD_DIM), HEAD_DIM)

    whole = pl.ds(0, heads * HEAD_DIM)

    def move(kind, k, channels, src_start, dst_start, count, peer):
        return pltpu.make_async_remote_copy(
            src_ref=win.at[:, pl.ds(src_start, count), channels],
            dst_ref=win.at[:, pl.ds(dst_start, count), channels],
            send_sem=send_sem.at[kind],
            recv_sem=recv_sem.at[kind, k],
            device_id=peer,
            device_id_type=MESH,
        )

    def flow(kind, k, channels):
        at = pl.multiple_of
        if kind == OUT:
            return move(kind, k, channels, at(BLOCK + core * CELL, CELL),
                        at(BLOCK + TOKENS + core * CELL, CELL), CELL, (outside, col))
        if kind == SIB:
            return move(kind, k, channels, at(BLOCK + far * CELL, CELL),
                        at(BLOCK + TOKENS + far * CELL, CELL), CELL, (sibling, col))
        if kind == LEFT:
            return move(kind, k, channels, BLOCK, 0, TOKENS, (row, col + 1))
        if kind == RIGHT:
            return move(kind, k, channels, BLOCK, 2 * BLOCK, TOKENS, (row, col - 1))
        if kind == OUT_LEFT:
            return move(kind, k, channels, at(BLOCK + out_slot, CELL), out_slot, CELL, (row, col + 1))
        if kind == OUT_RIGHT:
            return move(kind, k, channels, at(BLOCK + out_slot, CELL), at(2 * BLOCK + out_slot, CELL), CELL, (row, col - 1))
        if kind == SIB_LEFT:
            return move(kind, k, channels, at(far * CELL, CELL), at(TOKENS + far * CELL, CELL), CELL, (sibling, col))
        return move(kind, k, channels, at(2 * BLOCK + far * CELL, CELL),
                    at(2 * BLOCK + TOKENS + far * CELL, CELL), CELL, (sibling, col))

    sends_if = {
        OUT: has_out, SIB: None, LEFT: has_right, RIGHT: has_left,
        OUT_LEFT: has_out & has_right, OUT_RIGHT: has_out & has_left,
        SIB_LEFT: has_left, SIB_RIGHT: has_right,
    }
    gets_if = {
        OUT: has_out, SIB: None, LEFT: has_left, RIGHT: has_right,
        OUT_LEFT: has_out & has_left, OUT_RIGHT: has_out & has_right,
        SIB_LEFT: has_left, SIB_RIGHT: has_right,
    }

    def when(cond, action):
        if cond is None:
            action()
        else:
            pl.when(cond)(action)

    def send(kind, k):
        when(sends_if[kind], lambda: flow(kind, k, lanes(k)).start())

    def get(kind, k):
        when(gets_if[kind], lambda: flow(kind, k, lanes(k)).wait_recv())

    @pl.loop(0, heads)
    def _(k):
        for kind in (OUT, LEFT, RIGHT, SIB):
            send(kind, k)

    def clear(start, count):
        win[:, pl.ds(start, count), :] = jnp.zeros((4, count, heads * HEAD_DIM), win.dtype)

    @pl.when(jnp.logical_not(has_left))
    def _():
        clear(0, BLOCK)

    @pl.when(jnp.logical_not(has_right))
    def _():
        clear(2 * BLOCK, BLOCK)

    @pl.when(jnp.logical_not(has_out))
    def _():
        for block in range(3):
            clear(pl.multiple_of(block * BLOCK + out_slot, CELL), CELL)

    for dr, dc, there in around:
        slot = (dr + 1) * 3 + dc + 1

        @pl.when(jnp.logical_not(there))
        def _():
            stat_in[slot] = jnp.zeros(stat_in.shape[1:], stat_in.dtype)

    fill_bias(bias, row, col, rows * TILE_ROWS, cols * TILE_COLS)

    scale = 1.0 / math.sqrt(HEAD_DIM)
    scale2 = scale / math.log(2.0)
    own = pl.ds(BLOCK, TOKENS)

    def stat_move(index, k, src, dst):
        dr, dc, _ = around[index]
        return pltpu.make_async_remote_copy(
            src_ref=src, dst_ref=dst,
            send_sem=stat_send.at[index], recv_sem=stat_recv.at[index, k],
            device_id=(row + dr, col + dc), device_id_type=MESH,
        )

    def forward(k):
        get(OUT, k)
        send(OUT_LEFT, k)
        send(OUT_RIGHT, k)
        get(LEFT, k)
        send(SIB_LEFT, k)
        get(RIGHT, k)
        send(SIB_RIGHT, k)

    def query_pass(k):
        for kind in (SIB, OUT_LEFT, OUT_RIGHT, SIB_LEFT, SIB_RIGHT):
            get(kind, k)
        channels = lanes(k)
        keys = win[1, :, channels]
        scores = dot(win[0, own, channels], keys, ((1,), (1,))) * scale2 + bias[...]
        peak = jnp.max(scores, axis=1, keepdims=True)
        weights = jnp.exp2(scores - peak)
        total = jnp.sum(weights, axis=1, keepdims=True)
        grad_prob = dot(win[3, own, channels], win[2, :, channels], ((1,), (1,)))
        inverse = 1.0 / total
        offset = jnp.sum(weights * grad_prob, axis=1, keepdims=True) * inverse
        grad_score = ((weights * inverse) * (grad_prob - offset)).astype(jnp.bfloat16)
        out_ref[:, channels] = (dot(grad_score, keys, ((1,), (0,))) * scale).astype(jnp.bfloat16)
        log_total = peak + jnp.log2(total)
        lane = lax.broadcasted_iota(jnp.int32, (TOKENS, TOKENS), 1)
        stats = jnp.where(lane == 0, log_total, jnp.where(lane == 1, offset, 0.0)).T[:8]
        stat_out[k] = stats
        stat_in[4, k] = stats
        for index, (dr, dc, there) in enumerate(around):
            slot = (1 - dr) * 3 + 1 - dc
            when(there, lambda: stat_move(index, k, stat_out.at[k], stat_in.at[slot, k]).start())

    def key_pass(k):
        for index, (dr, dc, there) in enumerate(around):
            when(there, lambda: stat_move(7 - index, k, stat_out.at[k], stat_in.at[(dr + 1) * 3 + dc + 1, k]).wait_recv())
        channels = lanes(k)
        lane = lax.broadcasted_iota(jnp.int32, (1, TOKENS), 1)
        totals, offsets = [], []
        for block in range(3):
            for which, parts in ((0, totals), (1, offsets)):
                parts.append(stat_in[3 + block, k, which : which + 1, :])
                parts.append(
                    jnp.where(
                        lane < CELL,
                        stat_in[6 + block, k, which : which + 1, :],
                        stat_in[block, k, which : which + 1, :],
                    )
                )
        log_total = jnp.concatenate(totals, axis=1)
        offset = jnp.concatenate(offsets, axis=1)
        queries, grads = win[0, :, channels], win[3, :, channels]
        scores = dot(win[1, own, channels], queries, ((1,), (1,))) * scale2 + bias[...]
        weights = jnp.exp2(scores - log_total)
        grad_prob = dot(win[2, own, channels], grads, ((1,), (1,)))
        grad_score = (weights * (grad_prob - offset)).astype(jnp.bfloat16)
        key_lanes = pl.ds(pl.multiple_of((heads + k) * HEAD_DIM, HEAD_DIM), HEAD_DIM)
        value_lanes = pl.ds(pl.multiple_of((2 * heads + k) * HEAD_DIM, HEAD_DIM), HEAD_DIM)
        out_ref[:, key_lanes] = (dot(grad_score, queries, ((1,), (0,))) * scale).astype(jnp.bfloat16)
        out_ref[:, value_lanes] = dot(weights.astype(jnp.bfloat16), grads, ((1,), (0,))).astype(jnp.bfloat16)

    look = min(LOOK, heads)

    @pl.loop(0, look)
    def _(k):
        forward(k)

    @pl.loop(0, heads)
    def _(k):
        @pl.when(k + look < heads)
        def _():
            forward(k + look)

        query_pass(k)

        @pl.when(k > 0)
        def _():
            key_pass(k - 1)

    key_pass(heads - 1)

    for kind in range(8):
        when(sends_if[kind], lambda: flow(kind, 0, whole).wait_send())
    for index, (dr, dc, there) in enumerate(around):
        when(there, lambda: stat_move(index, 0, stat_out, stat_in.at[0]).wait_send())


def per_device(queries, keys, values, out_grad):
    tile_rows, tile_cols, channels = queries.shape
    heads = channels // HEAD_DIM
    rows, cols = lax.axis_size("row"), lax.axis_size("col")
    flat = [x.reshape(TOKENS, channels) for x in (queries, keys, values, out_grad)]
    out = pl.pallas_call(
        functools.partial(kernel, heads, rows, cols),
        out_shape=jax.ShapeDtypeStruct((TOKENS, 3 * channels), jnp.bfloat16),
        in_specs=[pl.BlockSpec(memory_space=pl.ANY)] * 4,
        out_specs=pl.BlockSpec(memory_space=pltpu.VMEM),
        scratch_shapes=[
            pltpu.VMEM((4, WINDOW, channels), jnp.bfloat16),
            pltpu.VMEM((TOKENS, WINDOW), jnp.float32),
            pltpu.VMEM((heads, 8, TOKENS), jnp.float32),
            pltpu.VMEM((9, heads, 8, TOKENS), jnp.float32),
            pltpu.SemaphoreType.DMA((4,)),
            pltpu.SemaphoreType.DMA((8,)),
            pltpu.SemaphoreType.DMA((8, heads)),
            pltpu.SemaphoreType.DMA((8,)),
            pltpu.SemaphoreType.DMA((8, heads)),
        ],
        compiler_params=pltpu.CompilerParams(
            collective_id=0, has_side_effects=True, vmem_limit_bytes=40 * 1024 * 1024
        ),
        name="window_backward",
    )(*flat)
    return out.reshape(tile_rows, tile_cols, 3 * channels)


def solution(mesh):
    spec = P("row", "col", None)
    return jax.shard_map(
        per_device, mesh=mesh, in_specs=(spec,) * 4, out_specs=spec, check_vma=False
    )
```

```python
import functools
import math

import jax
import jax.numpy as jnp
from jax import lax
from jax.experimental import pallas as pl
from jax.experimental.pallas import tpu as pltpu
from jax.sharding import PartitionSpec as P

HEAD_DIM = 128
RADIUS = 8
TILE_ROWS = 16
TILE_COLS = 8
TOKENS = TILE_ROWS * TILE_COLS
CELL = 64
BLOCK = 2 * TOKENS
SPAN = 3 * BLOCK
GROUP = 4
BLOCKS = GROUP + 2
FLOOR = -1e30
MESH = pl.DeviceIdType.MESH


def dot(a, b, dims):
    return lax.dot_general(a, b, (dims, ((), ())), preferred_element_type=jnp.float32)


def fill_bias(bias, row, group, grid_rows, grid_cols):
    own = lax.broadcasted_iota(jnp.int32, (TOKENS, TOKENS), 0)
    lane = lax.broadcasted_iota(jnp.int32, (TOKENS, TOKENS), 1)
    own_row, own_col = own >> 3, own & 7

    @pl.loop(0, GROUP)
    def _(tile):
        for block in range(3):
            for half in range(2):
                if half == 0:
                    key_row = lane >> 3
                else:
                    key_row = jnp.where(lane < CELL, 16 + (lane >> 3), (lane >> 3) - 16)
                key_col = (lane & 7) + (block - 1) * TILE_COLS
                grid_row = key_row + row * TILE_ROWS
                grid_col = key_col + (group * GROUP + tile) * TILE_COLS
                ok = (
                    (jnp.abs(own_row - key_row) <= RADIUS)
                    & (jnp.abs(own_col - key_col) <= RADIUS)
                    & (grid_row >= 0)
                    & (grid_row < grid_rows)
                    & (grid_col >= 0)
                    & (grid_col < grid_cols)
                )
                start = block * BLOCK + half * TOKENS
                bias[tile, :, start : start + TOKENS] = jnp.where(ok, 0.0, FLOOR)


def both(*conditions):
    there = None
    for cond in conditions:
        if cond is not None:
            there = cond if there is None else there & cond
    return there


def when(cond, action):
    if cond is None:
        action()
    else:
        pl.when(cond)(action)


def kernel(
    heads, rows, cols,
    q_ref, k_ref, v_ref, g_ref, out_ref,
    mine, win, bias, stats, parts,
    load_sem, local_sem, share_send, share_recv, out_send, out_recv, col_send, col_recv,
    sib_send, sib_recv, stat_send, stat_recv, part_send, part_recv, part_local,
):
    per = heads // GROUP
    row, col = lax.axis_index("row"), lax.axis_index("col")
    core = lax.rem(row, 2)
    x = lax.rem(col, GROUP)
    group = col // GROUP
    first = group * GROUP
    outside = row - 1 + 2 * core
    sibling = row + 1 - 2 * core
    has_out = (outside >= 0) & (outside < rows)
    has_left = group > 0
    has_right = group < cols // GROUP - 1
    has_up = row > 0
    has_down = row < rows - 1
    has_row = {-1: has_up, 0: None, 1: has_down}

    loads = []
    for a, ref in enumerate((q_ref, k_ref, v_ref, g_ref)):
        copy = pltpu.make_async_copy(ref, mine.at[a], load_sem.at[a])
        copy.start()
        loads.append(copy)

    barrier = pltpu.get_barrier_semaphore()

    def greet(device):
        pl.semaphore_signal(barrier, inc=1, device_id=device, device_id_type=MESH)

    for step in range(1, GROUP):
        greet((row, first + lax.rem(x + step, GROUP)))
    greet((sibling, col))

    @pl.when(has_out)
    def _():
        for peer in range(GROUP):
            greet((outside, first + peer))

    for there, shift in ((has_left, -GROUP), (has_right, GROUP)):
        for dr in (-1, 0, 1):
            when(both(there, has_row[dr]), lambda: greet((row + dr, col + shift)))
    sides = has_left.astype(jnp.int32) + has_right.astype(jnp.int32)
    lines = 1 + has_up.astype(jnp.int32) + has_down.astype(jnp.int32)
    pl.semaphore_wait(barrier, GROUP + GROUP * has_out.astype(jnp.int32) + sides * lines)
    for copy in loads:
        copy.wait()

    far = 1 - core
    out_slot = pl.multiple_of(TOKENS + far * CELL, CELL)
    own_rows = pl.ds(0, TOKENS)
    width = per * HEAD_DIM

    def lanes(k):
        if isinstance(k, int):
            return pl.ds(k * HEAD_DIM, HEAD_DIM)
        return pl.ds(pl.multiple_of(k * HEAD_DIM, HEAD_DIM), HEAD_DIM)

    def remote(src, dst, send_sem, recv_sem, device):
        return pltpu.make_async_remote_copy(
            src_ref=src, dst_ref=dst, send_sem=send_sem, recv_sem=recv_sem,
            device_id=device, device_id_type=MESH,
        )

    def share(step, h):
        peer = lax.rem(x + step, GROUP)
        return remote(
            mine.at[:, :, lanes(per * peer + h)], win.at[:, x + 1, own_rows, lanes(h)],
            share_send.at[step], share_recv.at[step, h], (row, first + peer),
        )

    def keep(h):
        return pltpu.make_async_copy(
            mine.at[:, :, lanes(per * x + h)], win.at[:, x + 1, own_rows, lanes(h)], local_sem.at[h]
        )

    def outer(step, h):
        peer = lax.rem(x + step, GROUP)
        return remote(
            mine.at[:, pl.ds(pl.multiple_of(core * CELL, CELL), CELL), lanes(per * peer + h)],
            win.at[:, x + 1, pl.ds(pl.multiple_of(TOKENS + core * CELL, CELL), CELL), lanes(h)],
            out_send.at[step], out_recv.at[step, h], (outside, first + peer),
        )

    def column(kind, h):
        src, dst, shift = ((1, BLOCKS - 1, -GROUP), (GROUP, 0, GROUP))[kind % 2]
        piece = own_rows if kind < 2 else pl.ds(out_slot, CELL)
        return remote(
            win.at[:, src, piece, lanes(h)], win.at[:, dst, piece, lanes(h)],
            col_send.at[kind], col_recv.at[kind, h], (row, col + shift),
        )

    def beside(kind, h):
        start, count = ((1, GROUP), (0, 1), (BLOCKS - 1, 1))[kind]
        return remote(
            win.at[:, pl.ds(start, count), pl.ds(pl.multiple_of(far * CELL, CELL), CELL), lanes(h)],
            win.at[:, pl.ds(start, count), pl.ds(pl.multiple_of(TOKENS + far * CELL, CELL), CELL), lanes(h)],
            sib_send.at[kind], sib_recv.at[kind, h], (sibling, col),
        )

    notices = []
    for dr in (-1, 1):
        notices.append((dr, (1, GROUP), (1, GROUP), 0, has_row[dr], has_row[-dr]))
    for dr in (-1, 0, 1):
        notices.append((dr, (1, 1), (BLOCKS - 1, 1), -GROUP, both(has_left, has_row[dr]), both(has_right, has_row[-dr])))
        notices.append((dr, (GROUP, 1), (0, 1), GROUP, both(has_right, has_row[dr]), both(has_left, has_row[-dr])))

    def notice(index, h):
        dr, src, dst, shift, _, _ = notices[index]
        return remote(
            stats.at[1, h, pl.ds(*src)], stats.at[1 - dr, h, pl.ds(*dst)],
            stat_send.at[index], stat_recv.at[index, h], (row + dr, col + shift),
        )

    def start_share(h):
        keep(h).start()
        for step in range(1, GROUP):
            share(step, h).start()

    def start_outer(h):
        @pl.when(has_out)
        def _():
            for step in range(GROUP):
                outer(step, h).start()

    def spread_own(h):
        for step in range(1, GROUP):
            share(step, h).wait_recv()
        keep(h).wait()
        when(has_left, lambda: column(0, h).start())
        when(has_right, lambda: column(1, h).start())
        beside(0, h).start()

    def spread_outer(h):
        @pl.when(has_out)
        def _():
            for step in range(GROUP):
                outer(step, h).wait_recv()
            when(has_left, lambda: column(2, h).start())
            when(has_right, lambda: column(3, h).start())

    def complete(h):
        @pl.when(has_right)
        def _():
            column(0, h).wait_recv()
            beside(2, h).start()

        @pl.when(has_left)
        def _():
            column(1, h).wait_recv()
            beside(1, h).start()

        beside(0, h).wait_recv()
        when(both(has_right, has_out), lambda: column(2, h).wait_recv())
        when(both(has_left, has_out), lambda: column(3, h).wait_recv())
        when(has_right, lambda: beside(2, h).wait_recv())
        when(has_left, lambda: beside(1, h).wait_recv())

    start_outer(0)
    start_share(0)
    if per > 1:
        start_share(1)

    def clear(block, piece):
        win[:, block, piece, :] = jnp.zeros((4, piece.size, width), win.dtype)

    for there, block in ((has_left, 0), (has_right, BLOCKS - 1)):
        @pl.when(jnp.logical_not(there))
        def _():
            clear(block, pl.ds(0, BLOCK))
            for line in range(3):
                stats[line, :, block] = jnp.zeros((per, 8, TOKENS), stats.dtype)

    @pl.when(jnp.logical_not(has_out))
    def _():
        for block in range(BLOCKS):
            clear(block, pl.ds(out_slot, CELL))

    for dr in (-1, 1):
        @pl.when(jnp.logical_not(has_row[dr]))
        def _():
            stats[1 + dr] = jnp.zeros((per, BLOCKS, 8, TOKENS), stats.dtype)

    fill_bias(bias, row, group, rows * TILE_ROWS, cols * TILE_COLS)

    scale = 1.0 / math.sqrt(HEAD_DIM)
    scale2 = scale / math.log(2.0)

    def span(a, tile, h):
        return win[a, pl.ds(tile, 3), :, lanes(h)].reshape(SPAN, HEAD_DIM)

    def own(a, tile, h):
        return win[a, tile + 1, own_rows, lanes(h)]

    def deliver(which, tile, h, value):
        here = lanes(which * per + h)
        there = lanes(which * heads + per * x + h)
        parts[tile, :, here] = value.astype(parts.dtype)

        @pl.when(tile == x)
        def _():
            pltpu.make_async_copy(parts.at[tile, :, here], out_ref.at[:, there], part_local.at[0]).start()

        @pl.when(tile != x)
        def _():
            remote(
                parts.at[tile, :, here], out_ref.at[:, there],
                part_send.at[tile], part_recv.at[x], (row, first + tile),
            ).start()

    def query_pass(tile, h):
        keys = span(1, tile, h)
        scores = dot(own(0, tile, h), keys, ((1,), (1,))) * scale2 + bias[tile]
        peak = jnp.max(scores, axis=1, keepdims=True)
        weights = jnp.exp2(scores - peak)
        total = jnp.sum(weights, axis=1, keepdims=True)
        grad_prob = dot(own(3, tile, h), span(2, tile, h), ((1,), (1,)))
        inverse = 1.0 / total
        offset = jnp.sum(weights * grad_prob, axis=1, keepdims=True) * inverse
        grad_score = ((weights * inverse) * (grad_prob - offset)).astype(jnp.bfloat16)
        deliver(0, tile, h, dot(grad_score, keys, ((1,), (0,))) * scale)
        log_total = peak + jnp.log2(total)
        lane = lax.broadcasted_iota(jnp.int32, (TOKENS, TOKENS), 1)
        stats[1, h, tile + 1] = jnp.where(lane == 0, log_total, jnp.where(lane == 1, offset, 0.0)).T[:8]

    def key_pass(tile, h):
        lane = lax.broadcasted_iota(jnp.int32, (1, TOKENS), 1)

        def gather(which):
            pieces = []
            for block in range(3):
                here, above, below = (
                    stats[line, h, tile + block, which : which + 1, :] for line in (1, 0, 2)
                )
                pieces += [here, jnp.where(lane < CELL, below, above)]
            return jnp.concatenate(pieces, axis=1)

        log_total, offset = gather(0), gather(1)
        queries, grads = span(0, tile, h), span(3, tile, h)
        scores = dot(own(1, tile, h), queries, ((1,), (1,))) * scale2 + bias[tile]
        weights = jnp.exp2(scores - log_total)
        deliver(2, tile, h, dot(weights.astype(jnp.bfloat16), grads, ((1,), (0,))))
        grad_prob = dot(own(2, tile, h), grads, ((1,), (1,)))
        grad_score = (weights * (grad_prob - offset)).astype(jnp.bfloat16)
        deliver(1, tile, h, dot(grad_score, queries, ((1,), (0,))) * scale)

    def query_passes(h):
        @pl.loop(0, GROUP)
        def _(tile):
            query_pass(tile, h)

        for index in range(len(notices)):
            when(notices[index][4], lambda: notice(index, h).start())

    def key_passes(h):
        for index in range(len(notices)):
            when(notices[index][5], lambda: notice(index, h).wait_recv())

        @pl.loop(0, GROUP)
        def _(tile):
            key_pass(tile, h)

    spread_own(0)
    if per > 1:
        start_outer(1)
    if per > 2:
        start_share(2)
    spread_outer(0)
    for h in range(per):
        if h + 1 < per:
            spread_own(h + 1)
            if h + 2 < per:
                start_outer(h + 2)
            if h + 3 < per:
                start_share(h + 3)
        complete(h)
        query_passes(h)
        if h > 0:
            key_passes(h - 1)
        if h + 1 < per:
            spread_outer(h + 1)
    key_passes(per - 1)

    for step in range(1, GROUP):
        remote(
            win.at[:, 1, own_rows, :], win.at[:, 1, own_rows, :],
            share_send.at[step], share_recv.at[step, 0], (row, first + lax.rem(x + step, GROUP)),
        ).wait_send()

    def sent(block, piece, sem, recv, device):
        remote(win.at[:, block, piece, :], win.at[:, block, piece, :], sem, recv, device).wait_send()

    @pl.when(has_out)
    def _():
        for step in range(GROUP):
            sent(1, pl.ds(out_slot, CELL), out_send.at[step], out_recv.at[step, 0], (outside, col))

    for kind in range(4):
        side = (has_left, has_right)[kind % 2]
        shift = (-GROUP, GROUP)[kind % 2]
        piece = own_rows if kind < 2 else pl.ds(out_slot, CELL)
        when(
            side if kind < 2 else both(side, has_out),
            lambda: sent(1, piece, col_send.at[kind], col_recv.at[kind, 0], (row, col + shift)),
        )
    for kind, count, there in ((0, GROUP, None), (1, 1, has_left), (2, 1, has_right)):
        piece = win.at[:, pl.ds(0, count), pl.ds(0, CELL), :]
        when(there, lambda: remote(
            piece, piece, sib_send.at[kind], sib_recv.at[kind, 0], (sibling, col)
        ).wait_send())
    for index, (dr, src, _, shift, there, _) in enumerate(notices):
        piece = stats.at[1, :, pl.ds(*src)]
        when(there, lambda: remote(
            piece, piece, stat_send.at[index], stat_recv.at[index, 0], (row + dr, col + shift)
        ).wait_send())
    pltpu.make_async_copy(parts.at[0], parts.at[0], part_local.at[0]).wait()
    for peer in range(GROUP):
        @pl.when(peer != x)
        def _():
            copy = remote(parts.at[peer], parts.at[peer], part_send.at[peer], part_recv.at[peer], (row, first + peer))
            copy.wait_send()
            copy.wait_recv()


def per_device(queries, keys, values, out_grad):
    tile_rows, tile_cols, channels = queries.shape
    heads = channels // HEAD_DIM
    per = heads // GROUP
    rows, cols = lax.axis_size("row"), lax.axis_size("col")
    flat = [x.reshape(TOKENS, channels) for x in (queries, keys, values, out_grad)]
    dma = pltpu.SemaphoreType.DMA
    out = pl.pallas_call(
        functools.partial(kernel, heads, rows, cols),
        out_shape=jax.ShapeDtypeStruct((TOKENS, 3 * channels), jnp.bfloat16),
        in_specs=[pl.BlockSpec(memory_space=pl.ANY)] * 4,
        out_specs=pl.BlockSpec(memory_space=pltpu.VMEM),
        scratch_shapes=[
            pltpu.VMEM((4, TOKENS, channels), jnp.bfloat16),
            pltpu.VMEM((4, BLOCKS, BLOCK, per * HEAD_DIM), jnp.bfloat16),
            pltpu.VMEM((GROUP, TOKENS, SPAN), jnp.float32),
            pltpu.VMEM((3, per, BLOCKS, 8, TOKENS), jnp.float32),
            pltpu.VMEM((GROUP, TOKENS, 3 * per * HEAD_DIM), jnp.bfloat16),
            dma((4,)),
            dma((per,)),
            dma((GROUP,)),
            dma((GROUP, per)),
            dma((GROUP,)),
            dma((GROUP, per)),
            dma((4,)),
            dma((4, per)),
            dma((3,)),
            dma((3, per)),
            dma((8,)),
            dma((8, per)),
            dma((GROUP,)),
            dma((GROUP,)),
            dma((1,)),
        ],
        compiler_params=pltpu.CompilerParams(
            collective_id=0, has_side_effects=True, vmem_limit_bytes=60 * 1024 * 1024
        ),
        name="window_backward",
    )(*flat)
    return out.reshape(tile_rows, tile_cols, 3 * channels)


def solution(mesh):
    spec = P("row", "col", None)
    return jax.shard_map(
        per_device, mesh=mesh, in_specs=(spec,) * 4, out_specs=spec, check_vma=False
    )
```

```python
import functools
import math

import jax
import jax.numpy as jnp
from jax import lax
from jax.experimental import pallas as pl
from jax.experimental.pallas import tpu as pltpu
from jax.sharding import PartitionSpec as P

HEAD_DIM = 128
RADIUS = 8
TILE_ROWS = 16
TILE_COLS = 8
TOKENS = TILE_ROWS * TILE_COLS
CELL = 64
BLOCK = 2 * TOKENS
SPAN = 3 * BLOCK
KV = pl.ds(1, 2)
GROUP = 4
BLOCKS = GROUP + 2
FLOOR = -1e30
MESH = pl.DeviceIdType.MESH


def dot(a, b, dims):
    return lax.dot_general(a, b, (dims, ((), ())), preferred_element_type=jnp.float32)


def fill_bias(bias, row, group, grid_rows, grid_cols):
    line = lax.broadcasted_iota(jnp.int32, (TOKENS, TOKENS), 0)
    own = lax.broadcasted_iota(jnp.int32, (TOKENS, TOKENS), 1)
    own_row, own_col = own >> 3, own & 7

    @pl.loop(0, GROUP)
    def _(tile):
        for block in range(3):
            for half in range(2):
                if half == 0:
                    key_row = line >> 3
                else:
                    key_row = jnp.where(line < CELL, 16 + (line >> 3), (line >> 3) - 16)
                key_col = (line & 7) + (block - 1) * TILE_COLS
                grid_row = key_row + row * TILE_ROWS
                grid_col = key_col + (group * GROUP + tile) * TILE_COLS
                ok = (
                    (jnp.abs(own_row - key_row) <= RADIUS)
                    & (jnp.abs(own_col - key_col) <= RADIUS)
                    & (grid_row >= 0)
                    & (grid_row < grid_rows)
                    & (grid_col >= 0)
                    & (grid_col < grid_cols)
                )
                start = block * BLOCK + half * TOKENS
                bias[tile, start : start + TOKENS, :] = jnp.where(ok, 0.0, FLOOR)


def both(*conditions):
    there = None
    for cond in conditions:
        if cond is not None:
            there = cond if there is None else there & cond
    return there


def when(cond, action):
    if cond is None:
        action()
    else:
        pl.when(cond)(action)


def kernel(
    heads, rows, cols,
    q_ref, k_ref, v_ref, g_ref, out_ref,
    mine, win, bias, acc, sib_from, sib_to, col_from, col_to, out_from, out_to, parts,
    load_sem, local_sem, share_send, share_recv, out_send, out_recv, col_send, col_recv,
    sib_send, sib_recv, back_sib_send, back_sib_recv, back_col_send, back_col_recv,
    back_out_send, back_out_recv, part_send, part_recv, part_local,
):
    per = heads // GROUP
    row, col = lax.axis_index("row"), lax.axis_index("col")
    core = lax.rem(row, 2)
    x = lax.rem(col, GROUP)
    group = col // GROUP
    first = group * GROUP
    outside = row - 1 + 2 * core
    sibling = row + 1 - 2 * core
    has_out = (outside >= 0) & (outside < rows)
    has_left = group > 0
    has_right = group < cols // GROUP - 1
    loads = []
    for a, ref in enumerate((q_ref, k_ref, v_ref, g_ref)):
        copy = pltpu.make_async_copy(ref, mine.at[a], load_sem.at[a])
        copy.start()
        loads.append(copy)

    barrier = pltpu.get_barrier_semaphore()

    def greet(device):
        pl.semaphore_signal(barrier, inc=1, device_id=device, device_id_type=MESH)

    for step in range(1, GROUP):
        greet((row, first + lax.rem(x + step, GROUP)))
    greet((sibling, col))

    @pl.when(has_out)
    def _():
        for peer in range(GROUP):
            greet((outside, first + peer))

    for there, shift in ((has_left, -GROUP), (has_right, GROUP)):
        when(there, lambda: greet((row, col + shift)))
    sides = has_left.astype(jnp.int32) + has_right.astype(jnp.int32)
    pl.semaphore_wait(barrier, GROUP + GROUP * has_out.astype(jnp.int32) + sides)
    for copy in loads:
        copy.wait()

    far = 1 - core
    out_slot = pl.multiple_of(TOKENS + far * CELL, CELL)
    own_rows = pl.ds(0, TOKENS)
    width = per * HEAD_DIM

    def lanes(k):
        if isinstance(k, int):
            return pl.ds(k * HEAD_DIM, HEAD_DIM)
        return pl.ds(pl.multiple_of(k * HEAD_DIM, HEAD_DIM), HEAD_DIM)

    def remote(src, dst, send_sem, recv_sem, device):
        return pltpu.make_async_remote_copy(
            src_ref=src, dst_ref=dst, send_sem=send_sem, recv_sem=recv_sem,
            device_id=device, device_id_type=MESH,
        )

    def share(step, h):
        peer = lax.rem(x + step, GROUP)
        return remote(
            mine.at[:, :, lanes(per * peer + h)], win.at[:, x + 1, own_rows, lanes(h)],
            share_send.at[step], share_recv.at[step, h], (row, first + peer),
        )

    def keep(h):
        return pltpu.make_async_copy(
            mine.at[:, :, lanes(per * x + h)], win.at[:, x + 1, own_rows, lanes(h)], local_sem.at[h]
        )

    def outer(step, h):
        peer = lax.rem(x + step, GROUP)
        return remote(
            mine.at[KV, pl.ds(pl.multiple_of(core * CELL, CELL), CELL), lanes(per * peer + h)],
            win.at[KV, x + 1, pl.ds(pl.multiple_of(TOKENS + core * CELL, CELL), CELL), lanes(h)],
            out_send.at[step], out_recv.at[step, h], (outside, first + peer),
        )

    def column(kind, h):
        src, dst, shift = ((1, BLOCKS - 1, -GROUP), (GROUP, 0, GROUP))[kind % 2]
        piece = own_rows if kind < 2 else pl.ds(out_slot, CELL)
        return remote(
            win.at[KV, src, piece, lanes(h)], win.at[KV, dst, piece, lanes(h)],
            col_send.at[kind], col_recv.at[kind, h], (row, col + shift),
        )

    def beside(kind, h):
        start, count = ((1, GROUP), (0, 1), (BLOCKS - 1, 1))[kind]
        return remote(
            win.at[KV, pl.ds(start, count), pl.ds(pl.multiple_of(far * CELL, CELL), CELL), lanes(h)],
            win.at[KV, pl.ds(start, count), pl.ds(pl.multiple_of(TOKENS + far * CELL, CELL), CELL), lanes(h)],
            sib_send.at[kind], sib_recv.at[kind, h], (sibling, col),
        )

    def back_sib(h):
        return remote(sib_from.at[h], sib_to.at[h], back_sib_send.at[0], back_sib_recv.at[h], (sibling, col))

    def back_col(side, h):
        return remote(
            col_from.at[h, side], col_to.at[h, side],
            back_col_send.at[side], back_col_recv.at[side, h], (row, col + (-GROUP, GROUP)[side]),
        )

    def back_out(tile, h):
        return remote(
            out_from.at[h, tile], out_to.at[:, :, lanes(per * x + h)],
            back_out_send.at[tile], back_out_recv.at[x, h], (outside, first + tile),
        )

    def start_share(h):
        keep(h).start()
        for step in range(1, GROUP):
            share(step, h).start()

    def start_outer(h):
        @pl.when(has_out)
        def _():
            for step in range(GROUP):
                outer(step, h).start()

    def spread_own(h):
        for step in range(1, GROUP):
            share(step, h).wait_recv()
        keep(h).wait()
        when(has_left, lambda: column(0, h).start())
        when(has_right, lambda: column(1, h).start())
        beside(0, h).start()

    def spread_outer(h):
        @pl.when(has_out)
        def _():
            for step in range(GROUP):
                outer(step, h).wait_recv()
            when(has_left, lambda: column(2, h).start())
            when(has_right, lambda: column(3, h).start())

    def spread_edges(h):
        @pl.when(has_right)
        def _():
            column(0, h).wait_recv()
            beside(2, h).start()

        @pl.when(has_left)
        def _():
            column(1, h).wait_recv()
            beside(1, h).start()

    def complete_edges(h):
        when(both(has_right, has_out), lambda: column(2, h).wait_recv())
        when(both(has_left, has_out), lambda: column(3, h).wait_recv())
        when(has_right, lambda: beside(2, h).wait_recv())
        when(has_left, lambda: beside(1, h).wait_recv())

    def clear(block, piece):
        win[:, block, piece, :] = jnp.zeros((4, piece.size, width), win.dtype)

    def setup():
        for there, block in ((has_left, 0), (has_right, BLOCKS - 1)):
            @pl.when(jnp.logical_not(there))
            def _():
                clear(block, pl.ds(0, BLOCK))

        @pl.when(jnp.logical_not(has_out))
        def _():
            for block in range(BLOCKS):
                clear(block, pl.ds(out_slot, CELL))

        fill_bias(bias, row, group, rows * TILE_ROWS, cols * TILE_COLS)

        @pl.loop(0, per * 2 * BLOCKS)
        def _(i):
            acc[i // (2 * BLOCKS), lax.rem(i // BLOCKS, 2), lax.rem(i, BLOCKS)] = jnp.zeros(
                (BLOCK, HEAD_DIM), acc.dtype
            )

    scale = 1.0 / math.sqrt(HEAD_DIM)
    scale2 = scale / math.log(2.0)

    def span(a, tile, h):
        return win[a, pl.ds(tile, 3), :, lanes(h)].reshape(SPAN, HEAD_DIM)

    def own(a, tile, h):
        return win[a, tile + 1, own_rows, lanes(h)]

    def deliver(which, tile, h, value):
        here = lanes(which * per + h)
        there = lanes(which * heads + per * x + h)
        parts[tile, :, here] = value.astype(parts.dtype)

        @pl.when(tile == x)
        def _():
            pltpu.make_async_copy(parts.at[tile, :, here], out_ref.at[:, there], part_local.at[0]).start()

        @pl.when(tile != x)
        def _():
            remote(
                parts.at[tile, :, here], out_ref.at[:, there],
                part_send.at[tile], part_recv.at[x], (row, first + tile),
            ).start()

    def tile_pass(tile, h):
        keys = span(1, tile, h)
        queries, grads = own(0, tile, h), own(3, tile, h)
        scores = dot(keys, queries, ((1,), (1,))) * scale2 + bias[tile]
        peak = jnp.max(scores, axis=0, keepdims=True)
        weights = jnp.exp2(scores - peak)
        inverse = 1.0 / jnp.sum(weights, axis=0, keepdims=True)
        grad_prob = dot(span(2, tile, h), grads, ((1,), (1,)))
        offset = jnp.sum(weights * grad_prob, axis=0, keepdims=True) * inverse
        prob = weights * inverse
        grad_score = (prob * (grad_prob - offset)).astype(jnp.bfloat16)
        deliver(0, tile, h, dot(grad_score, keys, ((0,), (0,))) * scale)
        value_grad = dot(prob.astype(jnp.bfloat16), grads, ((1,), (0,)))
        key_grad = dot(grad_score, queries, ((1,), (0,))) * scale
        acc[h, 0, pl.ds(tile, 3)] += key_grad.reshape(3, BLOCK, HEAD_DIM)
        acc[h, 1, pl.ds(tile, 3)] += value_grad.reshape(3, BLOCK, HEAD_DIM)

    sib_slot = pl.multiple_of(TOKENS + core * CELL, CELL)
    far_rows = pl.ds(pl.multiple_of(far * CELL, CELL), CELL)
    out_rows = pl.ds(out_slot, CELL)

    def compute(h):
        beside(0, h).wait_recv()

        @pl.loop(1, GROUP - 1)
        def _(tile):
            tile_pass(tile, h)

        complete_edges(h)

        @pl.loop(0, 2)
        def _(edge):
            tile_pass((GROUP - 1) * edge, h)

        sib_from[h] = acc[h, :, :, pl.ds(sib_slot, CELL), :].astype(jnp.bfloat16)
        back_sib(h).start()

    def add_sibling(h):
        back_sib(h).wait_recv()
        acc[h, :, :, far_rows, :] += sib_to[h].astype(jnp.float32)
        for side, block, there in ((0, 0, has_left), (1, BLOCKS - 1, has_right)):
            @pl.when(there)
            def _():
                col_from[h, side, :, pl.ds(0, TOKENS), :] = acc[h, :, block, own_rows, :].astype(jnp.bfloat16)
                col_from[h, side, :, pl.ds(TOKENS, CELL), :] = acc[h, :, block, out_rows, :].astype(jnp.bfloat16)
                back_col(side, h).start()

    def add_sides(h):
        for side, block, there in ((0, GROUP, has_right), (1, 1, has_left)):
            @pl.when(there)
            def _():
                back_col(side, h).wait_recv()
                acc[h, :, block, own_rows, :] += col_to[h, side, :, pl.ds(0, TOKENS), :].astype(jnp.float32)
                acc[h, :, block, out_rows, :] += col_to[h, side, :, pl.ds(TOKENS, CELL), :].astype(jnp.float32)

        @pl.when(has_out)
        def _():
            for tile in range(GROUP):
                out_from[h, tile] = acc[h, :, tile + 1, out_rows, :].astype(jnp.bfloat16)
                back_out(tile, h).start()

        for tile in range(GROUP):
            for which in range(2):
                deliver(1 + which, tile, h, acc[h, which, tile + 1, own_rows, :])

    start_outer(0)
    start_share(0)
    start_outer(1)
    start_share(1)
    start_outer(2)
    start_share(2)
    setup()
    spread_own(0)
    spread_outer(0)
    spread_edges(0)
    spread_own(1)
    compute(0)
    spread_outer(1)
    spread_edges(1)
    spread_own(2)
    add_sibling(0)
    compute(1)
    add_sides(0)
    spread_outer(2)
    spread_edges(2)
    add_sibling(1)
    compute(2)
    add_sides(1)
    add_sibling(2)
    add_sides(2)

    for step in range(1, GROUP):
        remote(
            win.at[:, 1, own_rows, :], win.at[:, 1, own_rows, :],
            share_send.at[step], share_recv.at[step, 0], (row, first + lax.rem(x + step, GROUP)),
        ).wait_send()

    def sent(block, piece, sem, recv, device):
        remote(win.at[KV, block, piece, :], win.at[KV, block, piece, :], sem, recv, device).wait_send()

    @pl.when(has_out)
    def _():
        for step in range(GROUP):
            sent(1, pl.ds(out_slot, CELL), out_send.at[step], out_recv.at[step, 0], (outside, col))

    for kind in range(4):
        side = (has_left, has_right)[kind % 2]
        shift = (-GROUP, GROUP)[kind % 2]
        piece = own_rows if kind < 2 else pl.ds(out_slot, CELL)
        when(
            side if kind < 2 else both(side, has_out),
            lambda: sent(1, piece, col_send.at[kind], col_recv.at[kind, 0], (row, col + shift)),
        )
    for kind, count, there in ((0, GROUP, None), (1, 1, has_left), (2, 1, has_right)):
        piece = win.at[KV, pl.ds(0, count), pl.ds(0, CELL), :]
        when(there, lambda: remote(
            piece, piece, sib_send.at[kind], sib_recv.at[kind, 0], (sibling, col)
        ).wait_send())
    remote(sib_from, sib_to, back_sib_send.at[0], back_sib_recv.at[0], (sibling, col)).wait_send()
    for side, there in ((0, has_left), (1, has_right)):
        piece = col_from.at[:, side]
        when(there, lambda: remote(
            piece, piece, back_col_send.at[side], back_col_recv.at[side, 0], (row, col + (-GROUP, GROUP)[side])
        ).wait_send())
    pltpu.make_async_copy(parts.at[0], parts.at[0], part_local.at[0]).wait()
    for peer in range(GROUP):
        @pl.when(peer != x)
        def _():
            copy = remote(parts.at[peer], parts.at[peer], part_send.at[peer], part_recv.at[peer], (row, first + peer))
            copy.wait_send()
            copy.wait_recv()

    @pl.when(has_out)
    def _():
        for peer in range(GROUP):
            for h in range(per):
                remote(
                    out_from.at[h, 0], out_from.at[h, 0],
                    back_out_send.at[peer], back_out_recv.at[peer, h], (outside, col),
                ).wait_recv()
            remote(
                out_from.at[:, 0], out_from.at[:, 0],
                back_out_send.at[peer], back_out_recv.at[peer, 0], (outside, col),
            ).wait_send()
        edge = pl.ds(pl.multiple_of(core * CELL, CELL), CELL)
        for which in range(2):
            here = pl.ds((1 + which) * heads * HEAD_DIM, heads * HEAD_DIM)
            total = out_ref[edge, here].astype(jnp.float32) + out_to[which].astype(jnp.float32)
            out_ref[edge, here] = total.astype(jnp.bfloat16)


def per_device(queries, keys, values, out_grad):
    tile_rows, tile_cols, channels = queries.shape
    heads = channels // HEAD_DIM
    per = heads // GROUP
    rows, cols = lax.axis_size("row"), lax.axis_size("col")
    flat = [x.reshape(TOKENS, channels) for x in (queries, keys, values, out_grad)]
    dma = pltpu.SemaphoreType.DMA
    out = pl.pallas_call(
        functools.partial(kernel, heads, rows, cols),
        out_shape=jax.ShapeDtypeStruct((TOKENS, 3 * channels), jnp.bfloat16),
        in_specs=[pl.BlockSpec(memory_space=pl.ANY)] * 4,
        out_specs=pl.BlockSpec(memory_space=pltpu.VMEM),
        scratch_shapes=[
            pltpu.VMEM((4, TOKENS, channels), jnp.bfloat16),
            pltpu.VMEM((4, BLOCKS, BLOCK, per * HEAD_DIM), jnp.bfloat16),
            pltpu.VMEM((GROUP, SPAN, TOKENS), jnp.float32),
            pltpu.VMEM((per, 2, BLOCKS, BLOCK, HEAD_DIM), jnp.float32),
            pltpu.VMEM((per, 2, BLOCKS, CELL, HEAD_DIM), jnp.bfloat16),
            pltpu.VMEM((per, 2, BLOCKS, CELL, HEAD_DIM), jnp.bfloat16),
            pltpu.VMEM((per, 2, 2, TOKENS + CELL, HEAD_DIM), jnp.bfloat16),
            pltpu.VMEM((per, 2, 2, TOKENS + CELL, HEAD_DIM), jnp.bfloat16),
            pltpu.VMEM((per, GROUP, 2, CELL, HEAD_DIM), jnp.bfloat16),
            pltpu.VMEM((2, CELL, channels), jnp.bfloat16),
            pltpu.VMEM((GROUP, TOKENS, 3 * per * HEAD_DIM), jnp.bfloat16),
            dma((4,)),
            dma((per,)),
            dma((GROUP,)),
            dma((GROUP, per)),
            dma((GROUP,)),
            dma((GROUP, per)),
            dma((4,)),
            dma((4, per)),
            dma((3,)),
            dma((3, per)),
            dma((1,)),
            dma((per,)),
            dma((2,)),
            dma((2, per)),
            dma((GROUP,)),
            dma((GROUP, per)),
            dma((GROUP,)),
            dma((GROUP,)),
            dma((1,)),
        ],
        compiler_params=pltpu.CompilerParams(
            collective_id=0, has_side_effects=True, vmem_limit_bytes=60 * 1024 * 1024
        ),
        name="window_backward",
    )(*flat)
    return out.reshape(tile_rows, tile_cols, 3 * channels)


def solution(mesh):
    spec = P("row", "col", None)
    return jax.shard_map(
        per_device, mesh=mesh, in_specs=(spec,) * 4, out_specs=spec, check_vma=False
    )
```

```python
import functools
import math

import jax
import jax.numpy as jnp
from jax import lax
from jax.experimental import pallas as pl
from jax.experimental.pallas import tpu as pltpu
from jax.sharding import PartitionSpec as P

HEAD_DIM = 128
RADIUS = 8
TILE_ROWS = 16
TILE_COLS = 8
TOKENS = TILE_ROWS * TILE_COLS
CELL = 64
BLOCK = 2 * TOKENS
SPAN = 3 * BLOCK
KV = pl.ds(1, 2)
GROUP = 4
BLOCKS = GROUP + 2
FLOOR = -1e30
MESH = pl.DeviceIdType.MESH


def dot(a, b, dims):
    return lax.dot_general(a, b, (dims, ((), ())), preferred_element_type=jnp.float32)


def fill_bias(bias, row, group, grid_rows, grid_cols):
    line = lax.broadcasted_iota(jnp.int32, (TOKENS, TOKENS), 0)
    own = lax.broadcasted_iota(jnp.int32, (TOKENS, TOKENS), 1)
    own_row, own_col = own >> 3, own & 7

    @pl.loop(0, GROUP)
    def _(tile):
        for block in range(3):
            for half in range(2):
                if half == 0:
                    key_row = line >> 3
                else:
                    key_row = jnp.where(line < CELL, 16 + (line >> 3), (line >> 3) - 16)
                key_col = (line & 7) + (block - 1) * TILE_COLS
                grid_row = key_row + row * TILE_ROWS
                grid_col = key_col + (group * GROUP + tile) * TILE_COLS
                ok = (
                    (jnp.abs(own_row - key_row) <= RADIUS)
                    & (jnp.abs(own_col - key_col) <= RADIUS)
                    & (grid_row >= 0)
                    & (grid_row < grid_rows)
                    & (grid_col >= 0)
                    & (grid_col < grid_cols)
                )
                start = block * BLOCK + half * TOKENS
                bias[tile, start : start + TOKENS, :] = jnp.where(ok, 0.0, FLOOR)


def both(*conditions):
    there = None
    for cond in conditions:
        if cond is not None:
            there = cond if there is None else there & cond
    return there


def when(cond, action):
    if cond is None:
        action()
    else:
        pl.when(cond)(action)


def kernel(
    heads, rows, cols,
    q_ref, k_ref, v_ref, g_ref, out_ref,
    mine, win, bias, acc, sib_from, sib_to, col_from, col_to, out_from, out_to, parts,
    load_sem, local_sem, share_send, share_recv, out_send, out_recv, col_send, col_recv,
    sib_send, sib_recv, back_sib_send, back_sib_recv, back_col_send, back_col_recv,
    back_out_send, back_out_recv, part_send, part_recv, part_local,
):
    per = heads // GROUP
    row, col = lax.axis_index("row"), lax.axis_index("col")
    core = lax.rem(row, 2)
    x = lax.rem(col, GROUP)
    group = col // GROUP
    first = group * GROUP
    outside = row - 1 + 2 * core
    sibling = row + 1 - 2 * core
    has_out = (outside >= 0) & (outside < rows)
    has_left = group > 0
    has_right = group < cols // GROUP - 1
    loads = []
    for a, ref in enumerate((q_ref, k_ref, v_ref, g_ref)):
        copy = pltpu.make_async_copy(ref, mine.at[a], load_sem.at[a])
        copy.start()
        loads.append(copy)

    barrier = pltpu.get_barrier_semaphore()

    def greet(device):
        pl.semaphore_signal(barrier, inc=1, device_id=device, device_id_type=MESH)

    for step in range(1, GROUP):
        greet((row, first + lax.rem(x + step, GROUP)))
    greet((sibling, col))

    @pl.when(has_out)
    def _():
        for peer in range(GROUP):
            greet((outside, first + peer))

    for there, shift in ((has_left, -GROUP), (has_right, GROUP)):
        when(there, lambda: greet((row, col + shift)))
    sides = has_left.astype(jnp.int32) + has_right.astype(jnp.int32)
    pl.semaphore_wait(barrier, GROUP + GROUP * has_out.astype(jnp.int32) + sides)
    for copy in loads:
        copy.wait()

    far = 1 - core
    out_slot = pl.multiple_of(TOKENS + far * CELL, CELL)
    own_rows = pl.ds(0, TOKENS)
    width = per * HEAD_DIM

    def lanes(k):
        if isinstance(k, int):
            return pl.ds(k * HEAD_DIM, HEAD_DIM)
        return pl.ds(pl.multiple_of(k * HEAD_DIM, HEAD_DIM), HEAD_DIM)

    def remote(src, dst, send_sem, recv_sem, device):
        return pltpu.make_async_remote_copy(
            src_ref=src, dst_ref=dst, send_sem=send_sem, recv_sem=recv_sem,
            device_id=device, device_id_type=MESH,
        )

    def share(step, h):
        peer = lax.rem(x + step, GROUP)
        return remote(
            mine.at[:, :, lanes(per * peer + h)], win.at[:, x + 1, own_rows, lanes(h)],
            share_send.at[step], share_recv.at[step, h], (row, first + peer),
        )

    def keep(h):
        return pltpu.make_async_copy(
            mine.at[:, :, lanes(per * x + h)], win.at[:, x + 1, own_rows, lanes(h)], local_sem.at[h]
        )

    def outer(step, h):
        peer = lax.rem(x + step, GROUP)
        return remote(
            mine.at[KV, pl.ds(pl.multiple_of(core * CELL, CELL), CELL), lanes(per * peer + h)],
            win.at[KV, x + 1, pl.ds(pl.multiple_of(TOKENS + core * CELL, CELL), CELL), lanes(h)],
            out_send.at[step, h], out_recv.at[step, h], (outside, first + peer),
        )

    def column(kind, h):
        src, dst, shift = ((1, BLOCKS - 1, -GROUP), (GROUP, 0, GROUP))[kind % 2]
        piece = own_rows if kind < 2 else pl.ds(out_slot, CELL)
        return remote(
            win.at[KV, src, piece, lanes(h)], win.at[KV, dst, piece, lanes(h)],
            col_send.at[kind], col_recv.at[kind, h], (row, col + shift),
        )

    def beside(kind, h):
        start, count = ((1, GROUP), (0, 1), (BLOCKS - 1, 1))[kind]
        return remote(
            win.at[KV, pl.ds(start, count), pl.ds(pl.multiple_of(far * CELL, CELL), CELL), lanes(h)],
            win.at[KV, pl.ds(start, count), pl.ds(pl.multiple_of(TOKENS + far * CELL, CELL), CELL), lanes(h)],
            sib_send.at[kind], sib_recv.at[kind, h], (sibling, col),
        )

    def back_sib(h):
        return remote(sib_from.at[h], sib_to.at[h], back_sib_send.at[0], back_sib_recv.at[h], (sibling, col))

    def back_col(side, part, h):
        piece = (own_rows, pl.ds(TOKENS, CELL))[part]
        kind = 2 * side + part
        return remote(
            col_from.at[h, side, :, piece], col_to.at[h, side, :, piece],
            back_col_send.at[kind], back_col_recv.at[kind, h], (row, col + (-GROUP, GROUP)[side]),
        )

    def back_out(tile, h):
        return remote(
            out_from.at[h, tile], out_to.at[:, :, lanes(per * x + h)],
            back_out_send.at[tile], back_out_recv.at[x, h], (outside, first + tile),
        )

    def start_share(h):
        keep(h).start()
        for step in range(1, GROUP):
            share(step, h).start()

    def start_outer(h):
        @pl.when(has_out)
        def _():
            for step in range(GROUP):
                outer(step, h).start()

    def left_outer(h):
        @pl.when(has_out)
        def _():
            for step in range(GROUP):
                outer(step, h).wait_send()

    def spread_own(h):
        for step in range(1, GROUP):
            share(step, h).wait_recv()
        keep(h).wait()
        when(has_left, lambda: column(0, h).start())
        when(has_right, lambda: column(1, h).start())
        beside(0, h).start()

    def spread_outer(h):
        @pl.when(has_out)
        def _():
            for step in range(GROUP):
                outer(step, h).wait_recv()
            when(has_left, lambda: column(2, h).start())
            when(has_right, lambda: column(3, h).start())

    def spread_edges(h):
        @pl.when(has_right)
        def _():
            column(0, h).wait_recv()
            beside(2, h).start()

        @pl.when(has_left)
        def _():
            column(1, h).wait_recv()
            beside(1, h).start()

    def complete_edges(h):
        when(both(has_right, has_out), lambda: column(2, h).wait_recv())
        when(both(has_left, has_out), lambda: column(3, h).wait_recv())
        when(has_right, lambda: beside(2, h).wait_recv())
        when(has_left, lambda: beside(1, h).wait_recv())

    def clear(block, piece):
        win[:, block, piece, :] = jnp.zeros((4, piece.size, width), win.dtype)

    def setup():
        for there, block in ((has_left, 0), (has_right, BLOCKS - 1)):
            @pl.when(jnp.logical_not(there))
            def _():
                clear(block, pl.ds(0, BLOCK))

        @pl.when(jnp.logical_not(has_out))
        def _():
            for block in range(BLOCKS):
                clear(block, pl.ds(out_slot, CELL))

        fill_bias(bias, row, group, rows * TILE_ROWS, cols * TILE_COLS)

        @pl.loop(0, per * 2 * BLOCKS)
        def _(i):
            acc[i // (2 * BLOCKS), lax.rem(i // BLOCKS, 2), lax.rem(i, BLOCKS)] = jnp.zeros(
                (BLOCK, HEAD_DIM), acc.dtype
            )

    scale = 1.0 / math.sqrt(HEAD_DIM)
    scale2 = scale / math.log(2.0)

    def span(a, tile, h):
        return win[a, pl.ds(tile, 3), :, lanes(h)].reshape(SPAN, HEAD_DIM)

    def own(a, tile, h):
        return win[a, tile + 1, own_rows, lanes(h)]

    def deliver(which, tile, h, value):
        here = lanes(which * per + h)
        there = lanes(which * heads + per * x + h)
        parts[tile, :, here] = value.astype(parts.dtype)

        @pl.when(tile == x)
        def _():
            pltpu.make_async_copy(parts.at[tile, :, here], out_ref.at[:, there], part_local.at[0]).start()

        @pl.when(tile != x)
        def _():
            remote(
                parts.at[tile, :, here], out_ref.at[:, there],
                part_send.at[tile], part_recv.at[x], (row, first + tile),
            ).start()

    def tile_pass(tile, h):
        keys = span(1, tile, h)
        queries, grads = own(0, tile, h), own(3, tile, h)
        scores = dot(keys, queries, ((1,), (1,))) * scale2 + bias[tile]
        peak = jnp.max(scores, axis=0, keepdims=True)
        weights = jnp.exp2(scores - peak)
        inverse = 1.0 / jnp.sum(weights, axis=0, keepdims=True)
        grad_prob = dot(span(2, tile, h), grads, ((1,), (1,)))
        offset = jnp.sum(weights * grad_prob, axis=0, keepdims=True) * inverse
        prob = weights * inverse
        grad_score = (prob * (grad_prob - offset)).astype(jnp.bfloat16)
        deliver(0, tile, h, dot(grad_score, keys, ((0,), (0,))) * scale)
        value_grad = dot(prob.astype(jnp.bfloat16), grads, ((1,), (0,)))
        key_grad = dot(grad_score, queries, ((1,), (0,))) * scale
        acc[h, 0, pl.ds(tile, 3)] += key_grad.reshape(3, BLOCK, HEAD_DIM)
        acc[h, 1, pl.ds(tile, 3)] += value_grad.reshape(3, BLOCK, HEAD_DIM)

    sib_slot = pl.multiple_of(TOKENS + core * CELL, CELL)
    far_rows = pl.ds(pl.multiple_of(far * CELL, CELL), CELL)
    out_rows = pl.ds(out_slot, CELL)

    sides_from = ((0, 0, has_left), (1, BLOCKS - 1, has_right))
    sides_to = ((0, GROUP, has_right), (1, 1, has_left))

    def compute(h):
        beside(0, h).wait_recv()

        @pl.loop(1, GROUP - 1)
        def _(tile):
            tile_pass(tile, h)

        complete_edges(h)

        @pl.loop(0, 2)
        def _(edge):
            tile_pass((GROUP - 1) * edge, h)

        @pl.when(has_out)
        def _():
            for side, block, there in sides_from:
                @pl.when(there)
                def _():
                    col_from[h, side, :, pl.ds(TOKENS, CELL), :] = acc[h, :, block, out_rows, :].astype(jnp.bfloat16)
                    back_col(side, 1, h).start()
            for tile in range(1, GROUP - 1):
                out_from[h, tile] = acc[h, :, tile + 1, out_rows, :].astype(jnp.bfloat16)
                back_out(tile, h).start()

        sib_from[h] = acc[h, :, :, pl.ds(sib_slot, CELL), :].astype(jnp.bfloat16)
        back_sib(h).start()

    def add_sibling(h):
        back_sib(h).wait_recv()
        acc[h, :, :, far_rows, :] += sib_to[h].astype(jnp.float32)
        for side, block, there in sides_from:
            @pl.when(there)
            def _():
                col_from[h, side, :, own_rows, :] = acc[h, :, block, own_rows, :].astype(jnp.bfloat16)
                back_col(side, 0, h).start()

    def add_outer(h):
        @pl.when(has_out)
        def _():
            for side, block, there in sides_to:
                @pl.when(there)
                def _():
                    back_col(side, 1, h).wait_recv()
                    acc[h, :, block, out_rows, :] += col_to[h, side, :, pl.ds(TOKENS, CELL), :].astype(jnp.float32)
                out_from[h, block - 1] = acc[h, :, block, out_rows, :].astype(jnp.bfloat16)
                back_out(block - 1, h).start()

    def add_sides(h):
        for side, block, there in sides_to:
            @pl.when(there)
            def _():
                back_col(side, 0, h).wait_recv()
                acc[h, :, block, own_rows, :] += col_to[h, side, :, own_rows, :].astype(jnp.float32)
        for tile in range(GROUP):
            for which in range(2):
                deliver(1 + which, tile, h, acc[h, which, tile + 1, own_rows, :])

    start_outer(0)
    start_share(0)
    start_outer(1)
    start_share(1)
    start_outer(2)
    start_share(2)
    setup()
    spread_own(0)
    spread_outer(0)
    spread_own(1)
    spread_edges(0)
    spread_outer(1)
    compute(0)
    spread_own(2)
    spread_edges(1)
    spread_outer(2)
    compute(1)
    add_outer(0)
    add_sibling(0)
    spread_edges(2)
    compute(2)
    add_outer(1)
    add_sibling(1)
    add_outer(2)
    add_sibling(2)
    add_sides(0)
    add_sides(1)
    add_sides(2)
    for h in range(per):
        left_outer(h)

    for step in range(1, GROUP):
        remote(
            win.at[:, 1, own_rows, :], win.at[:, 1, own_rows, :],
            share_send.at[step], share_recv.at[step, 0], (row, first + lax.rem(x + step, GROUP)),
        ).wait_send()

    def sent(block, piece, sem, recv, device):
        remote(win.at[KV, block, piece, :], win.at[KV, block, piece, :], sem, recv, device).wait_send()

    for kind in range(4):
        side = (has_left, has_right)[kind % 2]
        shift = (-GROUP, GROUP)[kind % 2]
        piece = own_rows if kind < 2 else pl.ds(out_slot, CELL)
        when(
            side if kind < 2 else both(side, has_out),
            lambda: sent(1, piece, col_send.at[kind], col_recv.at[kind, 0], (row, col + shift)),
        )
    for kind, count, there in ((0, GROUP, None), (1, 1, has_left), (2, 1, has_right)):
        piece = win.at[KV, pl.ds(0, count), pl.ds(0, CELL), :]
        when(there, lambda: remote(
            piece, piece, sib_send.at[kind], sib_recv.at[kind, 0], (sibling, col)
        ).wait_send())
    remote(sib_from, sib_to, back_sib_send.at[0], back_sib_recv.at[0], (sibling, col)).wait_send()
    for side, _, there in sides_from:
        for part, cond in ((0, there), (1, there & has_out)):
            piece = col_from.at[:, side, :, (own_rows, pl.ds(TOKENS, CELL))[part]]
            when(cond, lambda: remote(
                piece, piece, back_col_send.at[2 * side + part], back_col_recv.at[2 * side + part, 0],
                (row, col + (-GROUP, GROUP)[side]),
            ).wait_send())
    pltpu.make_async_copy(parts.at[0], parts.at[0], part_local.at[0]).wait()
    for peer in range(GROUP):
        @pl.when(peer != x)
        def _():
            copy = remote(parts.at[peer], parts.at[peer], part_send.at[peer], part_recv.at[peer], (row, first + peer))
            copy.wait_send()
            copy.wait_recv()

    @pl.when(has_out)
    def _():
        for peer in range(GROUP):
            for h in range(per):
                remote(
                    out_from.at[h, 0], out_from.at[h, 0],
                    back_out_send.at[peer], back_out_recv.at[peer, h], (outside, col),
                ).wait_recv()
            remote(
                out_from.at[:, 0], out_from.at[:, 0],
                back_out_send.at[peer], back_out_recv.at[peer, 0], (outside, col),
            ).wait_send()
        edge = pl.ds(pl.multiple_of(core * CELL, CELL), CELL)
        for which in range(2):
            here = pl.ds((1 + which) * heads * HEAD_DIM, heads * HEAD_DIM)
            total = out_ref[edge, here].astype(jnp.float32) + out_to[which].astype(jnp.float32)
            out_ref[edge, here] = total.astype(jnp.bfloat16)


def per_device(queries, keys, values, out_grad):
    tile_rows, tile_cols, channels = queries.shape
    heads = channels // HEAD_DIM
    per = heads // GROUP
    rows, cols = lax.axis_size("row"), lax.axis_size("col")
    flat = [x.reshape(TOKENS, channels) for x in (queries, keys, values, out_grad)]
    dma = pltpu.SemaphoreType.DMA
    out = pl.pallas_call(
        functools.partial(kernel, heads, rows, cols),
        out_shape=jax.ShapeDtypeStruct((TOKENS, 3 * channels), jnp.bfloat16),
        in_specs=[pl.BlockSpec(memory_space=pl.ANY)] * 4,
        out_specs=pl.BlockSpec(memory_space=pltpu.VMEM),
        scratch_shapes=[
            pltpu.VMEM((4, TOKENS, channels), jnp.bfloat16),
            pltpu.VMEM((4, BLOCKS, BLOCK, per * HEAD_DIM), jnp.bfloat16),
            pltpu.VMEM((GROUP, SPAN, TOKENS), jnp.float32),
            pltpu.VMEM((per, 2, BLOCKS, BLOCK, HEAD_DIM), jnp.float32),
            pltpu.VMEM((per, 2, BLOCKS, CELL, HEAD_DIM), jnp.bfloat16),
            pltpu.VMEM((per, 2, BLOCKS, CELL, HEAD_DIM), jnp.bfloat16),
            pltpu.VMEM((per, 2, 2, TOKENS + CELL, HEAD_DIM), jnp.bfloat16),
            pltpu.VMEM((per, 2, 2, TOKENS + CELL, HEAD_DIM), jnp.bfloat16),
            pltpu.VMEM((per, GROUP, 2, CELL, HEAD_DIM), jnp.bfloat16),
            pltpu.VMEM((2, CELL, channels), jnp.bfloat16),
            pltpu.VMEM((GROUP, TOKENS, 3 * per * HEAD_DIM), jnp.bfloat16),
            dma((4,)),
            dma((per,)),
            dma((GROUP,)),
            dma((GROUP, per)),
            dma((GROUP, per)),
            dma((GROUP, per)),
            dma((4,)),
            dma((4, per)),
            dma((3,)),
            dma((3, per)),
            dma((1,)),
            dma((per,)),
            dma((4,)),
            dma((4, per)),
            dma((GROUP,)),
            dma((GROUP, per)),
            dma((GROUP,)),
            dma((GROUP,)),
            dma((1,)),
        ],
        compiler_params=pltpu.CompilerParams(
            collective_id=0, has_side_effects=True, vmem_limit_bytes=60 * 1024 * 1024
        ),
        name="window_backward",
    )(*flat)
    return out.reshape(tile_rows, tile_cols, 3 * channels)


def solution(mesh):
    spec = P("row", "col", None)
    return jax.shard_map(
        per_device, mesh=mesh, in_specs=(spec,) * 4, out_specs=spec, check_vma=False
    )
```

```python
import functools
import math

import jax
import jax.numpy as jnp
from jax import lax
from jax.experimental import pallas as pl
from jax.experimental.pallas import tpu as pltpu
from jax.sharding import PartitionSpec as P

HEAD_DIM = 128
RADIUS = 8
TILE_ROWS = 16
TILE_COLS = 8
TOKENS = TILE_ROWS * TILE_COLS
CELL = 64
BLOCK = 2 * TOKENS
SPAN = 3 * BLOCK
KV, QG = pl.ds(0, 2), pl.ds(2, 2)
GROUP = 4
BLOCKS = GROUP + 2
FLOOR = -1e30
MESH = pl.DeviceIdType.MESH


def dot(a, b, dims):
    return lax.dot_general(a, b, (dims, ((), ())), preferred_element_type=jnp.float32)


def fill_bias(bias, row, group, grid_rows, grid_cols):
    line = lax.broadcasted_iota(jnp.int32, (TOKENS, TOKENS), 0)
    own = lax.broadcasted_iota(jnp.int32, (TOKENS, TOKENS), 1)
    own_row, own_col = own >> 3, own & 7

    @pl.loop(0, GROUP)
    def _(tile):
        for block in range(3):
            for half in range(2):
                if half == 0:
                    key_row = line >> 3
                else:
                    key_row = jnp.where(line < CELL, 16 + (line >> 3), (line >> 3) - 16)
                key_col = (line & 7) + (block - 1) * TILE_COLS
                grid_row = key_row + row * TILE_ROWS
                grid_col = key_col + (group * GROUP + tile) * TILE_COLS
                ok = (
                    (jnp.abs(own_row - key_row) <= RADIUS)
                    & (jnp.abs(own_col - key_col) <= RADIUS)
                    & (grid_row >= 0)
                    & (grid_row < grid_rows)
                    & (grid_col >= 0)
                    & (grid_col < grid_cols)
                )
                start = block * BLOCK + half * TOKENS
                bias[tile, start : start + TOKENS, :] = jnp.where(ok, 0.0, FLOOR)


def both(*conditions):
    there = None
    for cond in conditions:
        if cond is not None:
            there = cond if there is None else there & cond
    return there


def when(cond, action):
    if cond is None:
        action()
    else:
        pl.when(cond)(action)


def kernel(
    heads, rows, cols,
    q_ref, k_ref, v_ref, g_ref, out_ref,
    mine, win, bias, acc, sib_from, sib_to, col_from, col_to, out_from, out_to, parts,
    load_sem, local_sem, share_send, share_recv, out_send, out_recv, col_send, col_recv,
    sib_send, sib_recv, back_sib_send, back_sib_recv, back_col_send, back_col_recv,
    back_out_send, back_out_recv, part_send, part_recv, part_local,
):
    per = heads // GROUP
    row, col = lax.axis_index("row"), lax.axis_index("col")
    core = lax.rem(row, 2)
    x = lax.rem(col, GROUP)
    group = col // GROUP
    first = group * GROUP
    outside = row - 1 + 2 * core
    sibling = row + 1 - 2 * core
    has_out = (outside >= 0) & (outside < rows)
    has_left = group > 0
    has_right = group < cols // GROUP - 1
    loads = []
    for a, ref in enumerate((k_ref, v_ref, q_ref, g_ref)):
        copy = pltpu.make_async_copy(ref, mine.at[a], load_sem.at[a])
        copy.start()
        loads.append(copy)

    barrier = pltpu.get_barrier_semaphore()

    def greet(device):
        pl.semaphore_signal(barrier, inc=1, device_id=device, device_id_type=MESH)

    for step in range(1, GROUP):
        greet((row, first + lax.rem(x + step, GROUP)))
    greet((sibling, col))

    @pl.when(has_out)
    def _():
        for peer in range(GROUP):
            greet((outside, first + peer))

    for there, shift in ((has_left, -GROUP), (has_right, GROUP)):
        when(there, lambda: greet((row, col + shift)))
    sides = has_left.astype(jnp.int32) + has_right.astype(jnp.int32)
    pl.semaphore_wait(barrier, GROUP + GROUP * has_out.astype(jnp.int32) + sides)
    for copy in loads:
        copy.wait()

    far = 1 - core
    out_slot = pl.multiple_of(TOKENS + far * CELL, CELL)
    own_rows = pl.ds(0, TOKENS)
    width = per * HEAD_DIM

    def lanes(k):
        if isinstance(k, int):
            return pl.ds(k * HEAD_DIM, HEAD_DIM)
        return pl.ds(pl.multiple_of(k * HEAD_DIM, HEAD_DIM), HEAD_DIM)

    def remote(src, dst, send_sem, recv_sem, device):
        return pltpu.make_async_remote_copy(
            src_ref=src, dst_ref=dst, send_sem=send_sem, recv_sem=recv_sem,
            device_id=device, device_id_type=MESH,
        )

    def share(step, h, part):
        peer = lax.rem(x + step, GROUP)
        return remote(
            mine.at[(KV, QG)[part], :, lanes(per * peer + h)], win.at[(KV, QG)[part], x + 1, own_rows, lanes(h)],
            share_send.at[step], share_recv.at[step, 2 * h + part], (row, first + peer),
        )

    def keep(h):
        return pltpu.make_async_copy(
            mine.at[:, :, lanes(per * x + h)], win.at[:, x + 1, own_rows, lanes(h)], local_sem.at[h]
        )

    def outer(step, h):
        peer = lax.rem(x + step, GROUP)
        return remote(
            mine.at[KV, pl.ds(pl.multiple_of(core * CELL, CELL), CELL), lanes(per * peer + h)],
            win.at[KV, x + 1, pl.ds(pl.multiple_of(TOKENS + core * CELL, CELL), CELL), lanes(h)],
            out_send.at[step, h], out_recv.at[step, h], (outside, first + peer),
        )

    def column(kind, h):
        src, dst, shift = ((1, BLOCKS - 1, -GROUP), (GROUP, 0, GROUP))[kind % 2]
        piece = own_rows if kind < 2 else pl.ds(out_slot, CELL)
        return remote(
            win.at[KV, src, piece, lanes(h)], win.at[KV, dst, piece, lanes(h)],
            col_send.at[kind], col_recv.at[kind, h], (row, col + shift),
        )

    def beside(kind, h):
        start, count = ((1, GROUP), (0, 1), (BLOCKS - 1, 1))[kind]
        return remote(
            win.at[KV, pl.ds(start, count), pl.ds(pl.multiple_of(far * CELL, CELL), CELL), lanes(h)],
            win.at[KV, pl.ds(start, count), pl.ds(pl.multiple_of(TOKENS + far * CELL, CELL), CELL), lanes(h)],
            sib_send.at[kind], sib_recv.at[kind, h], (sibling, col),
        )

    def back_sib(h):
        return remote(sib_from.at[h], sib_to.at[h], back_sib_send.at[0], back_sib_recv.at[h], (sibling, col))

    def back_col(side, part, h):
        piece = (own_rows, pl.ds(TOKENS, CELL))[part]
        kind = 2 * side + part
        return remote(
            col_from.at[h, side, :, piece], col_to.at[h, side, :, piece],
            back_col_send.at[kind], back_col_recv.at[kind, h], (row, col + (-GROUP, GROUP)[side]),
        )

    def back_out(tile, h):
        return remote(
            out_from.at[h, tile], out_to.at[:, :, lanes(per * x + h)],
            back_out_send.at[tile], back_out_recv.at[x, h], (outside, first + tile),
        )

    def start_share(h, part):
        if part == 0:
            keep(h).start()
        for step in range(1, GROUP):
            share(step, h, part).start()

    def start_outer(h):
        @pl.when(has_out)
        def _():
            for step in range(GROUP):
                outer(step, h).start()

    def left_outer(h):
        @pl.when(has_out)
        def _():
            for step in range(GROUP):
                outer(step, h).wait_send()

    def spread_own(h):
        for step in range(1, GROUP):
            share(step, h, 0).wait_recv()
        keep(h).wait()
        when(has_left, lambda: column(0, h).start())
        when(has_right, lambda: column(1, h).start())
        beside(0, h).start()

    def spread_outer(h):
        @pl.when(has_out)
        def _():
            for step in range(GROUP):
                outer(step, h).wait_recv()
            when(has_left, lambda: column(2, h).start())
            when(has_right, lambda: column(3, h).start())

    def spread_edges(h):
        @pl.when(has_right)
        def _():
            column(0, h).wait_recv()
            beside(2, h).start()

        @pl.when(has_left)
        def _():
            column(1, h).wait_recv()
            beside(1, h).start()

    def complete_edges(h):
        when(both(has_right, has_out), lambda: column(2, h).wait_recv())
        when(both(has_left, has_out), lambda: column(3, h).wait_recv())
        when(has_right, lambda: beside(2, h).wait_recv())
        when(has_left, lambda: beside(1, h).wait_recv())

    def clear(block, piece):
        win[:, block, piece, :] = jnp.zeros((4, piece.size, width), win.dtype)

    def setup():
        for there, block in ((has_left, 0), (has_right, BLOCKS - 1)):
            @pl.when(jnp.logical_not(there))
            def _():
                clear(block, pl.ds(0, BLOCK))

        @pl.when(jnp.logical_not(has_out))
        def _():
            for block in range(BLOCKS):
                clear(block, pl.ds(out_slot, CELL))

        fill_bias(bias, row, group, rows * TILE_ROWS, cols * TILE_COLS)

        @pl.loop(0, per * 2 * BLOCKS)
        def _(i):
            acc[i // (2 * BLOCKS), lax.rem(i // BLOCKS, 2), lax.rem(i, BLOCKS)] = jnp.zeros(
                (BLOCK, HEAD_DIM), acc.dtype
            )

    scale = 1.0 / math.sqrt(HEAD_DIM)
    scale2 = scale / math.log(2.0)

    def span(a, tile, h):
        return win[a, pl.ds(tile, 3), :, lanes(h)].reshape(SPAN, HEAD_DIM)

    def own(a, tile, h):
        return win[a, tile + 1, own_rows, lanes(h)]

    def deliver(which, tile, h, value):
        here = lanes(which * per + h)
        there = lanes(which * heads + per * x + h)
        parts[tile, :, here] = value.astype(parts.dtype)

        @pl.when(tile == x)
        def _():
            pltpu.make_async_copy(parts.at[tile, :, here], out_ref.at[:, there], part_local.at[0]).start()

        @pl.when(tile != x)
        def _():
            remote(
                parts.at[tile, :, here], out_ref.at[:, there],
                part_send.at[tile], part_recv.at[x], (row, first + tile),
            ).start()

    def tile_pass(tile, h):
        keys = span(0, tile, h)
        queries, grads = own(2, tile, h), own(3, tile, h)
        scores = dot(keys, queries, ((1,), (1,))) * scale2 + bias[tile]
        peak = jnp.max(scores, axis=0, keepdims=True)
        weights = jnp.exp2(scores - peak)
        inverse = 1.0 / jnp.sum(weights, axis=0, keepdims=True)
        grad_prob = dot(span(1, tile, h), grads, ((1,), (1,)))
        offset = jnp.sum(weights * grad_prob, axis=0, keepdims=True) * inverse
        prob = weights * inverse
        grad_score = (prob * (grad_prob - offset)).astype(jnp.bfloat16)
        deliver(0, tile, h, dot(grad_score, keys, ((0,), (0,))) * scale)
        value_grad = dot(prob.astype(jnp.bfloat16), grads, ((1,), (0,)))
        key_grad = dot(grad_score, queries, ((1,), (0,))) * scale
        acc[h, 0, pl.ds(tile, 3)] += key_grad.reshape(3, BLOCK, HEAD_DIM)
        acc[h, 1, pl.ds(tile, 3)] += value_grad.reshape(3, BLOCK, HEAD_DIM)

    sib_slot = pl.multiple_of(TOKENS + core * CELL, CELL)
    far_rows = pl.ds(pl.multiple_of(far * CELL, CELL), CELL)
    out_rows = pl.ds(out_slot, CELL)

    sides_from = ((0, 0, has_left), (1, BLOCKS - 1, has_right))
    sides_to = ((0, GROUP, has_right), (1, 1, has_left))

    def compute(h):
        beside(0, h).wait_recv()
        for step in range(1, GROUP):
            share(step, h, 1).wait_recv()

        @pl.loop(1, GROUP - 1)
        def _(tile):
            tile_pass(tile, h)

        complete_edges(h)

        @pl.loop(0, 2)
        def _(edge):
            tile_pass((GROUP - 1) * edge, h)

        @pl.when(has_out)
        def _():
            for side, block, there in sides_from:
                @pl.when(there)
                def _():
                    col_from[h, side, :, pl.ds(TOKENS, CELL), :] = acc[h, :, block, out_rows, :].astype(jnp.bfloat16)
                    back_col(side, 1, h).start()
            for tile in range(1, GROUP - 1):
                out_from[h, tile] = acc[h, :, tile + 1, out_rows, :].astype(jnp.bfloat16)
                back_out(tile, h).start()

        sib_from[h] = acc[h, :, :, pl.ds(sib_slot, CELL), :].astype(jnp.bfloat16)
        back_sib(h).start()

    def add_sibling(h):
        back_sib(h).wait_recv()
        acc[h, :, :, far_rows, :] += sib_to[h].astype(jnp.float32)
        for side, block, there in sides_from:
            @pl.when(there)
            def _():
                col_from[h, side, :, own_rows, :] = acc[h, :, block, own_rows, :].astype(jnp.bfloat16)
                back_col(side, 0, h).start()

    def add_outer(h):
        @pl.when(has_out)
        def _():
            for side, block, there in sides_to:
                @pl.when(there)
                def _():
                    back_col(side, 1, h).wait_recv()
                    acc[h, :, block, out_rows, :] += col_to[h, side, :, pl.ds(TOKENS, CELL), :].astype(jnp.float32)
                out_from[h, block - 1] = acc[h, :, block, out_rows, :].astype(jnp.bfloat16)
                back_out(block - 1, h).start()

    def add_sides(h):
        for side, block, there in sides_to:
            @pl.when(there)
            def _():
                back_col(side, 0, h).wait_recv()
                acc[h, :, block, own_rows, :] += col_to[h, side, :, own_rows, :].astype(jnp.float32)
        for tile in range(GROUP):
            for which in range(2):
                deliver(1 + which, tile, h, acc[h, which, tile + 1, own_rows, :])

    start_outer(0)
    start_share(0, 0)
    start_outer(1)
    start_share(1, 0)
    start_outer(2)
    start_share(2, 0)
    start_share(0, 1)
    start_share(1, 1)
    start_share(2, 1)
    setup()
    spread_own(0)
    spread_own(1)
    spread_outer(0)
    spread_own(2)
    spread_edges(0)
    spread_outer(1)
    compute(0)
    spread_edges(1)
    spread_outer(2)
    compute(1)
    add_outer(0)
    add_sibling(0)
    spread_edges(2)
    compute(2)
    add_outer(1)
    add_sibling(1)
    add_outer(2)
    add_sibling(2)
    add_sides(0)
    add_sides(1)
    add_sides(2)
    for h in range(per):
        left_outer(h)

    for step in range(1, GROUP):
        remote(
            win.at[:, 1, own_rows, :], win.at[:, 1, own_rows, :],
            share_send.at[step], share_recv.at[step, 0], (row, first + lax.rem(x + step, GROUP)),
        ).wait_send()

    def sent(block, piece, sem, recv, device):
        remote(win.at[KV, block, piece, :], win.at[KV, block, piece, :], sem, recv, device).wait_send()

    for kind in range(4):
        side = (has_left, has_right)[kind % 2]
        shift = (-GROUP, GROUP)[kind % 2]
        piece = own_rows if kind < 2 else pl.ds(out_slot, CELL)
        when(
            side if kind < 2 else both(side, has_out),
            lambda: sent(1, piece, col_send.at[kind], col_recv.at[kind, 0], (row, col + shift)),
        )
    for kind, count, there in ((0, GROUP, None), (1, 1, has_left), (2, 1, has_right)):
        piece = win.at[KV, pl.ds(0, count), pl.ds(0, CELL), :]
        when(there, lambda: remote(
            piece, piece, sib_send.at[kind], sib_recv.at[kind, 0], (sibling, col)
        ).wait_send())
    remote(sib_from, sib_to, back_sib_send.at[0], back_sib_recv.at[0], (sibling, col)).wait_send()
    for side, _, there in sides_from:
        for part, cond in ((0, there), (1, there & has_out)):
            piece = col_from.at[:, side, :, (own_rows, pl.ds(TOKENS, CELL))[part]]
            when(cond, lambda: remote(
                piece, piece, back_col_send.at[2 * side + part], back_col_recv.at[2 * side + part, 0],
                (row, col + (-GROUP, GROUP)[side]),
            ).wait_send())
    pltpu.make_async_copy(parts.at[0], parts.at[0], part_local.at[0]).wait()
    for peer in range(GROUP):
        @pl.when(peer != x)
        def _():
            copy = remote(parts.at[peer], parts.at[peer], part_send.at[peer], part_recv.at[peer], (row, first + peer))
            copy.wait_send()
            copy.wait_recv()

    @pl.when(has_out)
    def _():
        for peer in range(GROUP):
            for h in range(per):
                remote(
                    out_from.at[h, 0], out_from.at[h, 0],
                    back_out_send.at[peer], back_out_recv.at[peer, h], (outside, col),
                ).wait_recv()
            remote(
                out_from.at[:, 0], out_from.at[:, 0],
                back_out_send.at[peer], back_out_recv.at[peer, 0], (outside, col),
            ).wait_send()
        edge = pl.ds(pl.multiple_of(core * CELL, CELL), CELL)
        for which in range(2):
            here = pl.ds((1 + which) * heads * HEAD_DIM, heads * HEAD_DIM)
            total = out_ref[edge, here].astype(jnp.float32) + out_to[which].astype(jnp.float32)
            out_ref[edge, here] = total.astype(jnp.bfloat16)


def per_device(queries, keys, values, out_grad):
    tile_rows, tile_cols, channels = queries.shape
    heads = channels // HEAD_DIM
    per = heads // GROUP
    rows, cols = lax.axis_size("row"), lax.axis_size("col")
    flat = [x.reshape(TOKENS, channels) for x in (queries, keys, values, out_grad)]
    dma = pltpu.SemaphoreType.DMA
    out = pl.pallas_call(
        functools.partial(kernel, heads, rows, cols),
        out_shape=jax.ShapeDtypeStruct((TOKENS, 3 * channels), jnp.bfloat16),
        in_specs=[pl.BlockSpec(memory_space=pl.ANY)] * 4,
        out_specs=pl.BlockSpec(memory_space=pltpu.VMEM),
        scratch_shapes=[
            pltpu.VMEM((4, TOKENS, channels), jnp.bfloat16),
            pltpu.VMEM((4, BLOCKS, BLOCK, per * HEAD_DIM), jnp.bfloat16),
            pltpu.VMEM((GROUP, SPAN, TOKENS), jnp.float32),
            pltpu.VMEM((per, 2, BLOCKS, BLOCK, HEAD_DIM), jnp.float32),
            pltpu.VMEM((per, 2, BLOCKS, CELL, HEAD_DIM), jnp.bfloat16),
            pltpu.VMEM((per, 2, BLOCKS, CELL, HEAD_DIM), jnp.bfloat16),
            pltpu.VMEM((per, 2, 2, TOKENS + CELL, HEAD_DIM), jnp.bfloat16),
            pltpu.VMEM((per, 2, 2, TOKENS + CELL, HEAD_DIM), jnp.bfloat16),
            pltpu.VMEM((per, GROUP, 2, CELL, HEAD_DIM), jnp.bfloat16),
            pltpu.VMEM((2, CELL, channels), jnp.bfloat16),
            pltpu.VMEM((GROUP, TOKENS, 3 * per * HEAD_DIM), jnp.bfloat16),
            dma((4,)),
            dma((per,)),
            dma((GROUP,)),
            dma((GROUP, 2 * per)),
            dma((GROUP, per)),
            dma((GROUP, per)),
            dma((4,)),
            dma((4, per)),
            dma((3,)),
            dma((3, per)),
            dma((1,)),
            dma((per,)),
            dma((4,)),
            dma((4, per)),
            dma((GROUP,)),
            dma((GROUP, per)),
            dma((GROUP,)),
            dma((GROUP,)),
            dma((1,)),
        ],
        compiler_params=pltpu.CompilerParams(
            collective_id=0, has_side_effects=True, vmem_limit_bytes=60 * 1024 * 1024
        ),
        name="window_backward",
    )(*flat)
    return out.reshape(tile_rows, tile_cols, 3 * channels)


def solution(mesh):
    spec = P("row", "col", None)
    return jax.shard_map(
        per_device, mesh=mesh, in_specs=(spec,) * 4, out_specs=spec, check_vma=False
    )
```
